256 devices in a mesh: eig: 16 (over y_lo, x, core), space: 16 (over z, y_hi).
Axes of the slice: x: 4, y: 4 (y_hi: 2, y_lo: 2; y = y_hi * 2 + y_lo), z: 8, core: 2. Of those that a mesh axis runs over, the one named last changes fastest.
Arguments:
- eigenvectors: float32 [2, 256, 4, 3, 64, 128], P(None, 'eig', None, None, 'space'), as said below
- gauge_links: float32 [2, 3, 3, 64, 128], P(None, None, None, 'space'), may hold values from -2.5 to 2.5
- separations: int32 [4], replicated, may hold values from 0 to 3, each once
Outputs:
- meson_fields: float32 [2, 4, 2, 2, 256, 256], P(None, None, None, None, 'space', 'eig')
The draws below stay inside these ranges and needn't reach their ends.
Inputs may be any that keep to these rules, and one draw needn't show every extreme that they name: `separations`: each value appears once. `eigenvectors`: entries of size about (196608) ** -0.25.
All inputs are finite; a program needn't handle non-finite values.
Results may differ from the reference program's by a relative error of at most 0.00016.
Values sent between devices are 32-bit elements; how exact they have to be, the bound alone decides.
No kernel may reach another device: no remote copies, remote signals or barrier semaphores. Data moves between devices by JAX's collectives and lax.ppermute only.
A program may use at most 192 MiB of HBM per device.

```python
import jax
import jax.numpy as jnp
from jax import lax

NEIG = 256
NZD = 4
XY = 128
NZ = 64


def draw_eigenvectors(key, part):
    key = jax.random.fold_in(key, 11)
    spread = (24.0 * NZ * XY) ** (-0.25)
    values = jnp.clip(jax.random.normal(key, (2, NEIG, 4, 3, NZ, XY), jnp.float32), -6.0, 6.0)
    return values * spread


def block_scale(stream_key, dims, pieces, least, high):
    gain = 1.0
    for dim, shards_of in pieces:
        draws = jax.random.uniform(jax.random.fold_in(jax.random.fold_in(stream_key, 6), dim), (shards_of,), jnp.float32, least / len(pieces), high / len(pieces))
        gain = gain * jnp.repeat(jnp.exp(draws), dims[dim] // shards_of).reshape((-1,) + (1,) * (len(dims) - 1 - dim))
    return gain


def centred(key, shape, width, limit, cuts=(), held_as=jnp.bfloat16):
    level = block_scale(key, shape, cuts, -0.22, 0.18) if cuts else 1.0
    drawn = jax.random.normal(key, shape, jnp.float32) * width * level
    return jnp.minimum(jnp.maximum(drawn, -limit), limit).astype(held_as)


def setup_inputs(seed: int = 0) -> dict:
    key_of = jax.random.split(jax.random.key(seed), 4)
    return {
        "eigenvectors": draw_eigenvectors(jax.random.fold_in(key_of[3], 71), 0),
        "gauge_links": centred(key_of[1], (2, 3, 3, NZ, XY), 0.4, 2.5, ((3, 16),), jnp.float32),
        "separations": jax.random.permutation(key_of[2], NZD).astype(jnp.int32),
    }


highest = lax.Precision.HIGHEST


def colour_step(link_real, link_imag, vector_field, adjoint):
    real_rows = []
    imag_rows = []
    for colour_out in range(3):
        total_real = jnp.zeros_like(vector_field[0, :, :, 0])
        total_imag = jnp.zeros_like(vector_field[0, :, :, 0])
        for colour_in in range(3):
            if adjoint:
                entry_real = link_real[colour_in, colour_out]
                entry_imag = -link_imag[colour_in, colour_out]
            else:
                entry_real = link_real[colour_out, colour_in]
                entry_imag = link_imag[colour_out, colour_in]
            source_real = vector_field[0, :, :, colour_in]
            source_imag = vector_field[1, :, :, colour_in]
            total_real = total_real + entry_real * source_real - entry_imag * source_imag
            total_imag = total_imag + entry_real * source_imag + entry_imag * source_real
        real_rows.append(total_real)
        imag_rows.append(total_imag)
    return jnp.stack([jnp.stack(real_rows, axis=2), jnp.stack(imag_rows, axis=2)])


def spin_mix(eigen_block):
    swapped = jnp.concatenate([eigen_block[:, :, 2:], eigen_block[:, :, :2]], axis=2)
    chiral = jnp.concatenate([eigen_block[:, :, :2], -eigen_block[:, :, 2:]], axis=2)
    return jnp.stack([swapped, chiral])


def pair_terms(mixed_block, transported):
    products = jnp.einsum("gaisczx,kdjsczx->kgadji", mixed_block, transported, precision=highest)
    real_part = products[:, :, 0, 0] + products[:, :, 1, 1]
    imag_part = products[:, :, 0, 1] - products[:, :, 1, 0]
    return jnp.stack([real_part, imag_part], axis=2)


def reference(eigenvectors, gauge_links, separations):
    link_real = gauge_links[0]
    link_imag = gauge_links[1]
    mixed_block = spin_mix(eigenvectors)
    forward = eigenvectors
    backward = eigenvectors
    plus_terms = []
    minus_terms = []
    for length in range(NZD):
        forward = colour_step(link_real, link_imag, jnp.roll(forward, -1, axis=4), False)
        backward = jnp.roll(colour_step(link_real, link_imag, backward, True), 1, axis=4)
        plus_terms.append(pair_terms(mixed_block, forward[None]))
        minus_terms.append(pair_terms(mixed_block, backward[None]))
    meson_all = jnp.stack([jnp.concatenate(plus_terms, axis=0), jnp.concatenate(minus_terms, axis=0)])
    return jnp.swapaxes(jnp.take(meson_all, separations, axis=1), 4, 5)
```

```python
import jax
import jax.numpy as jnp
from jax import lax
from jax.experimental import pallas as pl
from jax.experimental.pallas import tpu as pltpu
from jax.sharding import Mesh, PartitionSpec as P

EIG = ("ylo", "x", "core")
SPACE = ("z", "yhi")
PLANE = ("yhi", "ylo", "x")
SIZES = {"ylo": 2, "x": 4, "core": 2, "z": 8, "yhi": 2}

NZD = 4
LANES = 128
PIECE = 16
ROWS = 104


def roll(value, by):
    return pltpu.roll(value, by % LANES, value.ndim - 1)


def lanes_of(value):
    return lax.broadcasted_iota(jnp.int32, value.shape, value.ndim - 1)


def exchange_pieces(rows):
    piece = lanes_of(rows[0]) >> 4
    for bit in (1, 2, 4):
        upper = (piece & bit) != 0
        after = list(rows)
        for i in range(8):
            if i & bit == 0:
                low, high = rows[i], rows[i | bit]
                after[i] = jnp.where(upper, roll(high, 16 * bit), low)
                after[i | bit] = jnp.where(upper, high, roll(low, -16 * bit))
        rows = after
    return rows


def cut_kernel(place_ref, vectors_ref, links_ref, out_ref):
    for j in range(2):
        for colour in range(3):
            for half in range(2):
                def load(part, spin, plane):
                    first = (((part * 16 + half * 8) * 4 + spin) * 3 + colour) * 4 + plane
                    return vectors_ref[pl.ds(first, 8, stride=48), :]

                plus = [None] * 8
                minus = [None] * 8
                for plane in range(4):
                    upper_real, upper_imag = load(0, j, plane), load(1, j, plane)
                    lower_real, lower_imag = load(0, j + 2, plane), load(1, j + 2, plane)
                    plus[plane] = upper_real - lower_imag
                    plus[4 + plane] = upper_imag + lower_real
                    minus[plane] = upper_real + lower_imag
                    minus[4 + plane] = upper_imag - lower_real
                for sign, rows in ((0, plus), (1, minus)):
                    first = (sign * 3 + colour) * 16 + half * 8
                    for block, value in enumerate(exchange_pieces(rows)):
                        out_ref[j * 8 + block, first : first + 8, :] = value
    own = place_ref[0]
    row = lax.broadcasted_iota(jnp.int32, (8, LANES), 0)
    rows = []
    for part in range(2):
        for plane in range(4):
            mine = links_ref[pl.ds((part * 9 + own) * 4 + plane, 1), :]
            last = links_ref[(part * 9 + 8) * 4 + plane : (part * 9 + 8) * 4 + plane + 1, :]
            rows.append(jnp.where(row == 0, mine, last))
    for block, value in enumerate(exchange_pieces(rows)):
        out_ref[block, 96:104, :] = value
        out_ref[8 + block, 96:104, :] = value


def shifted(here, here_swapped, above, above_swapped, by):
    if by == 4:
        return above, above_swapped
    keep = ((lanes_of(here) >> 4) & 3) >= by
    return (
        roll(jnp.where(keep, here, above_swapped), -16 * by),
        roll(jnp.where(keep, here_swapped, above), -16 * by),
    )


def field_kernel(
    place_ref, own_ref, other_ref, above_ref, out_ref, a_hi, a_lo, r_hi, r_lo, f_hi, f_lo, link_ref
):
    cls = place_ref[1]
    real_half = lax.broadcasted_iota(jnp.int32, (1, LANES), 1) < 64

    for source, start in ((own_ref, cls * LANES), (other_ref, (1 - cls) * LANES)):
        start = pl.multiple_of(start, LANES)
        for sign in range(2):
            for half in range(2):
                for colour in range(3):
                    first = (sign * 3 + colour) * 16
                    value = source[half, :, first : first + 16, :].reshape(LANES, LANES)
                    swapped = roll(value, 64)
                    turned = jnp.where(real_half, -swapped, swapped)
                    column = (half * 3 + colour) * LANES
                    for held, hi_ref, lo_ref in ((value, a_hi, a_lo), (turned, r_hi, r_lo)):
                        hi = held.astype(jnp.bfloat16)
                        lo = (held - hi.astype(jnp.float32)).astype(jnp.bfloat16)
                        hi_ref[sign, pl.ds(start, LANES), column : column + LANES] = hi
                        lo_ref[sign, pl.ds(start, LANES), column : column + LANES] = lo

    def link_rows(source):
        entries = [source[i, 96:97, :] for i in range(8)] + [source[0, 97:98, :]]
        return [[entries[3 * i + j] for j in range(3)] for i in range(3)]

    links = [link_rows(own_ref.at[0]), link_rows(own_ref.at[1]), link_rows(above_ref)]
    swapped_links = [[[roll(e, 64) for e in line] for line in tile] for tile in links]
    for half in range(2):
        product = links[half]
        for by in range(1, NZD + 1):
            if by > 1:
                moved = [
                    [
                        shifted(
                            links[half][i][j],
                            swapped_links[half][i][j],
                            links[half + 1][i][j],
                            swapped_links[half + 1][i][j],
                            by - 1,
                        )
                        for j in range(3)
                    ]
                    for i in range(3)
                ]
                product = [
                    [
                        sum(
                            spread[i][m][0] * moved[m][j][0] + spread[i][m][1] * moved[m][j][1]
                            for m in range(3)
                        )
                        for j in range(3)
                    ]
                    for i in range(3)
                ]
            spread = []
            for i in range(3):
                line = []
                for j in range(3):
                    entry = product[i][j]
                    swapped = roll(entry, 64)
                    real = jnp.where(real_half, entry, swapped)
                    imag = jnp.where(real_half, -swapped, entry)
                    at = ((((by - 1) * 2 + half) * 3 + i) * 3 + j) * 2
                    link_ref[at : at + 1, :] = real
                    link_ref[at + 1 : at + 2, :] = imag
                    line.append((real, imag))
                spread.append(line)

    def transport(block, carry):
        row = pl.multiple_of(block * 16, 16)
        for sign in range(2):
            tiles = []
            swapped = []
            for source in (own_ref.at[0], own_ref.at[1], above_ref):
                line = [
                    source[block, (sign * 3 + c) * 16 : (sign * 3 + c) * 16 + 16, :]
                    for c in range(3)
                ]
                tiles.append(line)
                swapped.append([roll(value, 64) for value in line])
            for by in range(1, NZD + 1):
                for half in range(2):
                    moved = [
                        shifted(
                            tiles[half][c],
                            swapped[half][c],
                            tiles[half + 1][c],
                            swapped[half + 1][c],
                            by,
                        )
                        for c in range(3)
                    ]
                    for i in range(3):
                        total = None
                        for j in range(3):
                            at = ((((by - 1) * 2 + half) * 3 + i) * 3 + j) * 2
                            term = (
                                link_ref[at : at + 1, :] * moved[j][0]
                                + link_ref[at + 1 : at + 2, :] * moved[j][1]
                            )
                            total = term if total is None else total + term
                        hi = total.astype(jnp.bfloat16)
                        lo = (total - hi.astype(jnp.float32)).astype(jnp.bfloat16)
                        column = (half * 3 + i) * LANES
                        rows = pl.ds(pl.multiple_of((by - 1) * LANES + row, 16), 16)
                        f_hi[sign, rows, column : column + LANES] = hi
                        f_lo[sign, rows, column : column + LANES] = lo
        return carry

    lax.fori_loop(0, 8, transport, 0)

    def product_of(left, right):
        return lax.dot_general(
            left, right, (((1,), (1,)), ((), ())), preferred_element_type=jnp.float32
        )

    for sign in range(2):
        for part, (hi_ref, lo_ref) in enumerate(((a_hi, a_lo), (r_hi, r_lo))):
            total = product_of(f_hi[sign], hi_ref[1 - sign])
            total = total + product_of(f_hi[sign], lo_ref[1 - sign])
            total = total + product_of(f_lo[sign], hi_ref[1 - sign])
            for by in range(NZD):
                for block in range(8):
                    for half in range(2):
                        out_ref[half, block, by * 4 + sign * 2 + part] = total[
                            by * LANES + block * 16 : by * LANES + block * 16 + 16,
                            half * LANES : half * LANES + LANES,
                        ]


def gather_kernel(separations_ref, shares_ref, out_ref):
    fields = []
    for q in range(NZD):
        at = separations_ref[q] * 4
        sums = []
        for index in range(4):
            total = shares_ref[0, at + index]
            for source in range(1, 16):
                total = total + shares_ref[source, at + index]
            sums.append(total * 0.5)
        plus_real, plus_imag, minus_real, minus_imag = sums
        fields.append(
            [
                plus_imag - minus_imag,
                minus_real - plus_real,
                plus_real + minus_real,
                plus_imag + minus_imag,
            ]
        )
    for pair in range(2):
        for z, value in enumerate(exchange_pieces(fields[2 * pair] + fields[2 * pair + 1])):
            out_ref[z, pair] = value


def place_kernel(own_ref, mirror_ref, out_ref):
    padding = jnp.zeros((LANES - 32, LANES), jnp.float32)
    turned = jnp.concatenate([own_ref[0], own_ref[1], padding]).T
    for pair in range(2):
        for index in range(8):
            q = pair * 2 + index // 4
            g = (index // 2) % 2
            part = index % 2
            out_ref[0, q, g, part] = turned[
                index * 16 : index * 16 + 16, pair * 16 : pair * 16 + 16
            ]
            value = mirror_ref[pair, :, index * 16 : index * 16 + 16]
            out_ref[1, q, g, part] = -value if part else value


SMEM = pl.BlockSpec(memory_space=pltpu.SMEM)
VMEM = pl.BlockSpec(memory_space=pltpu.VMEM)


def call(kernel, shape, inputs, scratch=(), limit=32, flops=0):
    specs = [SMEM if value.dtype == jnp.int32 else VMEM for value in inputs]
    count = sum(value.size for value in inputs)
    return pl.pallas_call(
        kernel,
        out_shape=jax.ShapeDtypeStruct(shape, jnp.float32),
        in_specs=specs,
        out_specs=VMEM,
        scratch_shapes=list(scratch),
        compiler_params=pltpu.CompilerParams(vmem_limit_bytes=limit * 1024 * 1024),
        cost_estimate=pl.CostEstimate(flops=flops, bytes_accessed=count * 8, transcendentals=0),
    )(*inputs)


def local(eigenvectors, gauge_links, separations):
    cls = lax.axis_index("core")
    block = lax.axis_index(("ylo", "x"))
    place = jnp.stack([block, cls]).astype(jnp.int32)

    vectors = eigenvectors.reshape(1536, LANES)
    links = gauge_links.reshape(72, LANES)
    chunks = call(cut_kernel, (16, ROWS, LANES), (place, vectors, links))
    own = lax.all_to_all(chunks, PLANE, split_axis=0, concat_axis=0, tiled=True)
    own = own.reshape(2, 8, ROWS, LANES)
    other = lax.ppermute(own, "core", [(0, 1), (1, 0)])
    above = lax.ppermute(own[0], "z", [(i, (i - 1) % 8) for i in range(8)])

    held = jnp.bfloat16
    shares = call(
        field_kernel,
        (2, 8, 16, 16, LANES),
        (place, own, other, above),
        [
            pltpu.VMEM((2, 256, 768), held),
            pltpu.VMEM((2, 256, 768), held),
            pltpu.VMEM((2, 256, 768), held),
            pltpu.VMEM((2, 256, 768), held),
            pltpu.VMEM((2, 512, 768), held),
            pltpu.VMEM((2, 512, 768), held),
            pltpu.VMEM((144, LANES), jnp.float32),
        ],
        limit=48,
        flops=2 * 2 * 2 * 3 * 512 * 768 * 256,
    )
    shares = shares.reshape(16, 16, 16, LANES)
    shares = lax.all_to_all(shares, PLANE, split_axis=0, concat_axis=0, tiled=True)
    parts = call(gather_kernel, (8, 2, 16, LANES), (separations, shares))
    parts = lax.all_to_all(parts, "z", split_axis=0, concat_axis=0, tiled=True)
    block = jnp.sum(parts, axis=0)
    mirror = lax.ppermute(
        block, EIG + SPACE, [(e * 16 + s, s * 16 + e) for e in range(16) for s in range(16)]
    )
    return call(place_kernel, (2, NZD, 2, 2, 16, 16), (block, mirror))


def solution(mesh):
    fine = Mesh(mesh.devices.reshape([SIZES[name] for name in EIG + SPACE]), EIG + SPACE)
    return jax.shard_map(
        local,
        mesh=fine,
        in_specs=(
            P(None, EIG, None, None, SPACE, None),
            P(None, None, None, SPACE, None),
            P(),
        ),
        out_specs=P(None, None, None, None, SPACE, EIG),
        check_vma=False,
    )
```

```python
import jax
import jax.numpy as jnp
from jax import lax
from jax.experimental import pallas as pl
from jax.experimental.pallas import tpu as pltpu
from jax.sharding import Mesh, PartitionSpec as P

EIG = ("ylo", "x", "core")
SPACE = ("z", "yhi")
PLANE = ("yhi", "ylo", "x")
SIZES = {"ylo": 2, "x": 4, "core": 2, "z": 8, "yhi": 2}

NZD = 4
LANES = 128
PIECE = 16
ROWS = 104


def roll(value, by):
    return pltpu.roll(value, by % LANES, value.ndim - 1)


def lanes_of(value):
    return lax.broadcasted_iota(jnp.int32, value.shape, value.ndim - 1)


def exchange_pieces(rows):
    piece = lanes_of(rows[0]) >> 4
    for bit in (1, 2, 4):
        upper = (piece & bit) != 0
        after = list(rows)
        for i in range(8):
            if i & bit == 0:
                low, high = rows[i], rows[i | bit]
                after[i] = jnp.where(upper, roll(high, 16 * bit), low)
                after[i | bit] = jnp.where(upper, high, roll(low, -16 * bit))
        rows = after
    return rows


def cut_kernel(vectors_hbm, links_hbm, out_ref, vectors_ref, links_ref, arrived):
    copies = [
        pltpu.make_async_copy(vectors_hbm.at[rows], vectors_ref.at[rows], arrived.at[index])
        for index, rows in enumerate(pl.ds(i * 384, 384) for i in (0, 2, 1, 3))
    ]
    copies.append(pltpu.make_async_copy(links_hbm, links_ref, arrived.at[4]))
    for copy in copies:
        copy.start()
    for half in range(2):
        copies[2 * half].wait()
        copies[2 * half + 1].wait()
        for j in range(2):
            for colour in range(3):

                def load(part, spin, plane):
                    first = (((part * 16 + half * 8) * 4 + spin) * 3 + colour) * 4 + plane
                    return vectors_ref[pl.ds(first, 8, stride=48), :]

                plus = [None] * 8
                minus = [None] * 8
                for plane in range(4):
                    upper_real, upper_imag = load(0, j, plane), load(1, j, plane)
                    lower_real, lower_imag = load(0, j + 2, plane), load(1, j + 2, plane)
                    plus[plane] = upper_real - lower_imag
                    plus[4 + plane] = upper_imag + lower_real
                    minus[plane] = upper_real + lower_imag
                    minus[4 + plane] = upper_imag - lower_real
                both = [jnp.stack(pair) for pair in zip(plus, minus)]
                for block, value in enumerate(exchange_pieces(both)):
                    for sign in range(2):
                        first = (sign * 3 + colour) * 16 + half * 8
                        out_ref[j * 8 + block, first : first + 8, :] = value[sign]
    copies[4].wait()
    own = lax.axis_index(("ylo", "x"))
    row = lax.broadcasted_iota(jnp.int32, (8, LANES), 0)
    rows = []
    for part in range(2):
        for plane in range(4):
            mine = links_ref[pl.ds((part * 9 + own) * 4 + plane, 1), :]
            last = links_ref[(part * 9 + 8) * 4 + plane : (part * 9 + 8) * 4 + plane + 1, :]
            rows.append(jnp.where(row == 0, mine, last))
    for block, value in enumerate(exchange_pieces(rows)):
        out_ref[block, 96:104, :] = value
        out_ref[8 + block, 96:104, :] = value


def shifted(here, here_swapped, above, above_swapped, by):
    if by == 4:
        return above, above_swapped
    keep = ((lanes_of(here) >> 4) & 3) >= by
    return (
        roll(jnp.where(keep, here, above_swapped), -16 * by),
        roll(jnp.where(keep, here_swapped, above), -16 * by),
    )


def split(value):
    hi = value.astype(jnp.bfloat16)
    return hi, (value - hi.astype(jnp.float32)).astype(jnp.bfloat16)


def spread_link(entry):
    real_half = lanes_of(entry) < 64
    swapped = roll(entry, 64)
    return jnp.where(real_half, entry, swapped), jnp.where(real_half, -swapped, entry)


def link_rows(source):
    entries = [source[i, 96:97, :] for i in range(8)] + [source[0, 97:98, :]]
    return [[entries[3 * i + j] for j in range(3)] for i in range(3)]


def multiply_links(here_ref, above_ref, link_ref):
    here, above = link_rows(here_ref), link_rows(above_ref)
    here_swapped = [[roll(e, 64) for e in line] for line in here]
    above_swapped = [[roll(e, 64) for e in line] for line in above]
    product = here
    for by in range(1, NZD + 1):
        if by > 1:
            moved = [
                [
                    shifted(here[i][j], here_swapped[i][j], above[i][j], above_swapped[i][j], by - 1)
                    for j in range(3)
                ]
                for i in range(3)
            ]
            product = [
                [
                    sum(
                        factors[i][m][0] * moved[m][j][0] + factors[i][m][1] * moved[m][j][1]
                        for m in range(3)
                    )
                    for j in range(3)
                ]
                for i in range(3)
            ]
        factors = [[spread_link(e) for e in line] for line in product]
        for i in range(3):
            for j in range(3):
                at = ((by - 1) * 9 + i * 3 + j) * 2
                link_ref[at : at + 1, :] = factors[i][j][0]
                link_ref[at + 1 : at + 2, :] = factors[i][j][1]


def transport(here_ref, above_ref, link_ref, hi_ref, lo_ref):
    def one_block(block, carry):
        for sign in range(2):
            here, above, here_swapped, above_swapped = [], [], [], []
            for c in range(3):
                first = (sign * 3 + c) * 16
                here.append(here_ref[block, first : first + 16, :])
                above.append(above_ref[block, first : first + 16, :])
                here_swapped.append(roll(here[c], 64))
                above_swapped.append(roll(above[c], 64))
            for by in range(1, NZD + 1):
                rows = pl.ds(pl.multiple_of((by - 1) * LANES + block * 16, 16), 16)
                moved = [
                    shifted(here[c], here_swapped[c], above[c], above_swapped[c], by)
                    for c in range(3)
                ]
                for i in range(3):
                    total = None
                    for j in range(3):
                        at = ((by - 1) * 9 + i * 3 + j) * 2
                        term = (
                            link_ref[at : at + 1, :] * moved[j][0]
                            + link_ref[at + 1 : at + 2, :] * moved[j][1]
                        )
                        total = term if total is None else total + term
                    hi, lo = split(total)
                    hi_ref[sign, rows, i * LANES : i * LANES + LANES] = hi
                    lo_ref[sign, rows, i * LANES : i * LANES + LANES] = lo
        return carry

    lax.fori_loop(0, 8, one_block, 0, unroll=8)


def prepare_rows(source, half, start, refs):
    start = pl.multiple_of(start, LANES)
    for sign in range(2):
        for colour in range(3):
            first = (sign * 3 + colour) * 16
            value = source[half, :, first : first + 16, :].reshape(LANES, LANES)
            swapped = roll(value, 64)
            turned = jnp.where(lanes_of(value) < 64, -swapped, swapped)
            at = (sign, pl.ds(start, LANES), slice(colour * LANES, colour * LANES + LANES))
            refs[0][at], refs[1][at] = split(value)
            refs[2][at], refs[3][at] = split(turned)


def products(sign, part, rows, hi_ref, lo_ref):
    def product_of(left, right):
        return lax.dot_general(
            left, right, (((1,), (1,)), ((), ())), preferred_element_type=jnp.float32
        )

    rows_hi, rows_lo = rows[2 * part][1 - sign], rows[2 * part + 1][1 - sign]
    total = product_of(hi_ref[sign], rows_hi)
    total = total + product_of(hi_ref[sign], rows_lo)
    return total + product_of(lo_ref[sign], rows_hi)


def low_kernel(
    own_ref, other_ref, sum_ref, u0, u1, u2, u3, d0, d1, d2, d3, f_hi, f_lo, link_ref
):
    cls = lax.axis_index("core")
    down, up = (d0, d1, d2, d3), (u0, u1, u2, u3)
    multiply_links(own_ref.at[0], own_ref.at[1], link_ref)
    transport(own_ref.at[0], own_ref.at[1], link_ref, f_hi, f_lo)
    for source, start in ((own_ref, cls * LANES), (other_ref, (1 - cls) * LANES)):
        prepare_rows(source, 0, start, down)
        prepare_rows(source, 1, start, up)
    for sign in range(2):
        for part in range(2):
            sum_ref[sign, part] = products(sign, part, down, f_hi, f_lo)


def high_kernel(own_ref, above_ref, sum_ref, u0, u1, u2, u3, out_ref, f_hi, f_lo, link_ref):
    multiply_links(own_ref.at[1], above_ref, link_ref)
    transport(own_ref.at[1], above_ref, link_ref, f_hi, f_lo)
    for sign in range(2):
        for part in range(2):
            total = sum_ref[sign, part] + products(sign, part, (u0, u1, u2, u3), f_hi, f_lo)
            for by in range(NZD):
                for block in range(8):
                    for half in range(2):
                        out_ref[half, block, by * 4 + sign * 2 + part] = total[
                            by * LANES + block * 16 : by * LANES + block * 16 + 16,
                            half * LANES : half * LANES + LANES,
                        ]


def gather_kernel(separations_ref, shares_ref, out_ref):
    fields = []
    for q in range(NZD):
        at = separations_ref[q] * 4
        sums = []
        for index in range(4):
            total = shares_ref[0, at + index]
            for source in range(1, 16):
                total = total + shares_ref[source, at + index]
            sums.append(total * 0.5)
        plus_real, plus_imag, minus_real, minus_imag = sums
        fields.append(
            [
                plus_imag - minus_imag,
                minus_real - plus_real,
                plus_real + minus_real,
                plus_imag + minus_imag,
            ]
        )
    for pair in range(2):
        for z, value in enumerate(exchange_pieces(fields[2 * pair] + fields[2 * pair + 1])):
            out_ref[z, pair] = value


def place_kernel(own_ref, mirror_ref, out_ref):
    padding = jnp.zeros((LANES - 32, LANES), jnp.float32)
    turned = jnp.concatenate([own_ref[0], own_ref[1], padding]).T
    for pair in range(2):
        for index in range(8):
            q = pair * 2 + index // 4
            g = (index // 2) % 2
            part = index % 2
            out_ref[0, q, g, part] = turned[
                index * 16 : index * 16 + 16, pair * 16 : pair * 16 + 16
            ]
            value = mirror_ref[pair, :, index * 16 : index * 16 + 16]
            out_ref[1, q, g, part] = -value if part else value


SMEM = pl.BlockSpec(memory_space=pltpu.SMEM)
VMEM = pl.BlockSpec(memory_space=pltpu.VMEM)


def call(kernel, outs, inputs, scratch=(), limit=32, flops=0, space=VMEM):
    shapes = [jax.ShapeDtypeStruct(shape, held) for shape, held in outs]
    specs = [SMEM if value.dtype == jnp.int32 else space for value in inputs]
    count = sum(value.size for value in inputs)
    return pl.pallas_call(
        kernel,
        out_shape=shapes,
        in_specs=specs,
        out_specs=[VMEM] * len(outs),
        scratch_shapes=list(scratch),
        compiler_params=pltpu.CompilerParams(vmem_limit_bytes=limit * 1024 * 1024),
        cost_estimate=pl.CostEstimate(flops=flops, bytes_accessed=count * 4, transcendentals=0),
    )(*inputs)


F32, B16 = jnp.float32, jnp.bfloat16
FIELD_SCRATCH = (
    pltpu.VMEM((2, 512, 384), B16),
    pltpu.VMEM((2, 512, 384), B16),
    pltpu.VMEM((72, LANES), F32),
)
LOW_SCRATCH = (pltpu.VMEM((2, 256, 384), B16),) * 4 + FIELD_SCRATCH
FIELD_FLOPS = 2 * 2 * 2 * 3 * 512 * 384 * 256


def local(eigenvectors, gauge_links, separations):
    vectors = eigenvectors.reshape(1536, LANES)
    links = gauge_links.reshape(72, LANES)
    (chunks,) = call(
        cut_kernel,
        [((16, ROWS, LANES), F32)],
        (vectors, links),
        (
            pltpu.VMEM((1536, LANES), F32),
            pltpu.VMEM((72, LANES), F32),
            pltpu.SemaphoreType.DMA((5,)),
        ),
        space=pl.BlockSpec(memory_space=pltpu.HBM),
    )
    own = lax.all_to_all(chunks, PLANE, split_axis=0, concat_axis=0, tiled=True)
    own = own.reshape(2, 8, ROWS, LANES)
    above = lax.ppermute(own[0], "z", [(i, (i - 1) % 8) for i in range(8)])
    other = lax.ppermute(own, "core", [(0, 1), (1, 0)])

    low = call(
        low_kernel,
        [((2, 2, 512, 256), F32)] + [((2, 256, 384), B16)] * 4,
        (own, other),
        LOW_SCRATCH,
        flops=FIELD_FLOPS,
    )
    (shares,) = call(
        high_kernel,
        [((2, 8, 16, 16, LANES), F32)],
        (own, above, *low),
        FIELD_SCRATCH,
        flops=FIELD_FLOPS,
    )
    shares = shares.reshape(16, 16, 16, LANES)
    shares = lax.all_to_all(shares, PLANE, split_axis=0, concat_axis=0, tiled=True)
    (parts,) = call(gather_kernel, [((8, 2, 16, LANES), F32)], (separations, shares))
    parts = lax.all_to_all(parts, "z", split_axis=0, concat_axis=0, tiled=True)
    block = jnp.sum(parts, axis=0)
    mirror = lax.ppermute(
        block, EIG + SPACE, [(e * 16 + s, s * 16 + e) for e in range(16) for s in range(16)]
    )
    (fields,) = call(place_kernel, [((2, NZD, 2, 2, 16, 16), F32)], (block, mirror))
    return fields


def solution(mesh):
    fine = Mesh(mesh.devices.reshape([SIZES[name] for name in EIG + SPACE]), EIG + SPACE)
    return jax.shard_map(
        local,
        mesh=fine,
        in_specs=(
            P(None, EIG, None, None, SPACE, None),
            P(None, None, None, SPACE, None),
            P(),
        ),
        out_specs=P(None, None, None, None, SPACE, EIG),
        check_vma=False,
    )
```

```python
import jax
import jax.numpy as jnp
from jax import lax
from jax.experimental import pallas as pl
from jax.experimental.pallas import tpu as pltpu
from jax.sharding import Mesh, PartitionSpec as P

EIG = ("ylo", "x", "core")
SPACE = ("z", "yhi")
PLANE = ("yhi", "ylo", "x")
SIZES = {"ylo": 2, "x": 4, "core": 2, "z": 8, "yhi": 2}

NZD = 4
LANES = 128
PIECE = 16
ROWS = 104


def roll(value, by):
    return pltpu.roll(value, by % LANES, value.ndim - 1)


def lanes_of(value):
    return lax.broadcasted_iota(jnp.int32, value.shape, value.ndim - 1)


def exchange_pieces(rows):
    piece = lanes_of(rows[0]) >> 4
    for bit in (1, 2, 4):
        upper = (piece & bit) != 0
        after = list(rows)
        for i in range(8):
            if i & bit == 0:
                low, high = rows[i], rows[i | bit]
                after[i] = jnp.where(upper, roll(high, 16 * bit), low)
                after[i | bit] = jnp.where(upper, high, roll(low, -16 * bit))
        rows = after
    return rows


def cut_kernel(vectors_hbm, links_hbm, out_ref, vectors_ref, links_ref, arrived):
    copies = [
        pltpu.make_async_copy(vectors_hbm.at[rows], vectors_ref.at[rows], arrived.at[index])
        for index, rows in enumerate(pl.ds(i * 384, 384) for i in (0, 2, 1, 3))
    ]
    copies.append(pltpu.make_async_copy(links_hbm, links_ref, arrived.at[4]))
    for copy in copies:
        copy.start()
    for half in range(2):
        copies[2 * half].wait()
        copies[2 * half + 1].wait()
        for j in range(2):
            for colour in range(3):

                def load(part, spin, plane):
                    first = (((part * 16 + half * 8) * 4 + spin) * 3 + colour) * 4 + plane
                    return vectors_ref[pl.ds(first, 8, stride=48), :]

                plus = [None] * 8
                minus = [None] * 8
                for plane in range(4):
                    upper_real, upper_imag = load(0, j, plane), load(1, j, plane)
                    lower_real, lower_imag = load(0, j + 2, plane), load(1, j + 2, plane)
                    plus[plane] = upper_real - lower_imag
                    plus[4 + plane] = upper_imag + lower_real
                    minus[plane] = upper_real + lower_imag
                    minus[4 + plane] = upper_imag - lower_real
                both = [jnp.stack(pair) for pair in zip(plus, minus)]
                for block, value in enumerate(exchange_pieces(both)):
                    for sign in range(2):
                        first = (sign * 3 + colour) * 16 + half * 8
                        out_ref[j * 8 + block, first : first + 8, :] = value[sign]
    copies[4].wait()
    own = lax.axis_index(("ylo", "x"))
    row = lax.broadcasted_iota(jnp.int32, (8, LANES), 0)
    rows = []
    for part in range(2):
        for plane in range(4):
            mine = links_ref[pl.ds((part * 9 + own) * 4 + plane, 1), :]
            last = links_ref[(part * 9 + 8) * 4 + plane : (part * 9 + 8) * 4 + plane + 1, :]
            rows.append(jnp.where(row == 0, mine, last))
    for block, value in enumerate(exchange_pieces(rows)):
        out_ref[block, 96:104, :] = value
        out_ref[8 + block, 96:104, :] = value


def shifted(here, here_swapped, above, above_swapped, by):
    if by == 4:
        return above, above_swapped
    keep = ((lanes_of(here) >> 4) & 3) >= by
    return (
        roll(jnp.where(keep, here, above_swapped), -16 * by),
        roll(jnp.where(keep, here_swapped, above), -16 * by),
    )


def split(value):
    hi = value.astype(jnp.bfloat16)
    return hi, (value - hi.astype(jnp.float32)).astype(jnp.bfloat16)


def spread_link(entry):
    real_half = lanes_of(entry) < 64
    swapped = roll(entry, 64)
    return jnp.where(real_half, entry, swapped), jnp.where(real_half, -swapped, entry)


def link_rows(source):
    entries = [source[i, 96:97, :] for i in range(8)] + [source[0, 97:98, :]]
    return [[entries[3 * i + j] for j in range(3)] for i in range(3)]


def multiply_links(here_ref, above_ref, link_ref):
    here, above = link_rows(here_ref), link_rows(above_ref)
    here_swapped = [[roll(e, 64) for e in line] for line in here]
    above_swapped = [[roll(e, 64) for e in line] for line in above]
    product = here
    for by in range(1, NZD + 1):
        if by > 1:
            moved = [
                [
                    shifted(here[i][j], here_swapped[i][j], above[i][j], above_swapped[i][j], by - 1)
                    for j in range(3)
                ]
                for i in range(3)
            ]
            product = [
                [
                    sum(
                        factors[i][m][0] * moved[m][j][0] + factors[i][m][1] * moved[m][j][1]
                        for m in range(3)
                    )
                    for j in range(3)
                ]
                for i in range(3)
            ]
        factors = [[spread_link(e) for e in line] for line in product]
        for i in range(3):
            for j in range(3):
                at = ((by - 1) * 9 + i * 3 + j) * 2
                link_ref[at : at + 1, :] = factors[i][j][0]
                link_ref[at + 1 : at + 2, :] = factors[i][j][1]


def transport(here_ref, above_ref, link_ref, hi_ref, lo_ref):
    def one_block(block, carry):
        for sign in range(2):
            here, above, here_swapped, above_swapped = [], [], [], []
            for c in range(3):
                first = (sign * 3 + c) * 16
                here.append(here_ref[block, first : first + 16, :])
                above.append(above_ref[block, first : first + 16, :])
                here_swapped.append(roll(here[c], 64))
                above_swapped.append(roll(above[c], 64))
            for by in range(1, NZD + 1):
                rows = pl.ds(pl.multiple_of((by - 1) * LANES + block * 16, 16), 16)
                moved = [
                    shifted(here[c], here_swapped[c], above[c], above_swapped[c], by)
                    for c in range(3)
                ]
                for i in range(3):
                    total = None
                    for j in range(3):
                        at = ((by - 1) * 9 + i * 3 + j) * 2
                        term = (
                            link_ref[at : at + 1, :] * moved[j][0]
                            + link_ref[at + 1 : at + 2, :] * moved[j][1]
                        )
                        total = term if total is None else total + term
                    hi, lo = split(total)
                    hi_ref[sign, rows, i * LANES : i * LANES + LANES] = hi
                    lo_ref[sign, rows, i * LANES : i * LANES + LANES] = lo
        return carry

    lax.fori_loop(0, 8, one_block, 0, unroll=8)


def prepare_rows(source, half, start, refs):
    start = pl.multiple_of(start, LANES)
    for sign in range(2):
        for colour in range(3):
            first = (sign * 3 + colour) * 16
            value = source[half, :, first : first + 16, :].reshape(LANES, LANES)
            swapped = roll(value, 64)
            turned = jnp.where(lanes_of(value) < 64, -swapped, swapped)
            at = (sign, pl.ds(start, LANES), slice(colour * LANES, colour * LANES + LANES))
            refs[0][at], refs[1][at] = split(value)
            refs[2][at], refs[3][at] = split(turned)


def products(sign, part, rows, hi_ref, lo_ref):
    def product_of(left, right):
        return lax.dot_general(
            left, right, (((1,), (1,)), ((), ())), preferred_element_type=jnp.float32
        )

    rows_hi, rows_lo = rows[2 * part][1 - sign], rows[2 * part + 1][1 - sign]
    total = product_of(hi_ref[sign], rows_hi)
    total = total + product_of(hi_ref[sign], rows_lo)
    return total + product_of(lo_ref[sign], rows_hi)


def low_kernel(
    own_ref, other_ref, sum_ref, u0, u1, u2, u3, d0, d1, d2, d3, f_hi, f_lo, link_ref
):
    cls = lax.axis_index("core")
    down, up = (d0, d1, d2, d3), (u0, u1, u2, u3)
    multiply_links(own_ref.at[0], own_ref.at[1], link_ref)
    transport(own_ref.at[0], own_ref.at[1], link_ref, f_hi, f_lo)
    for source, start in ((own_ref, cls * LANES), (other_ref, (1 - cls) * LANES)):
        prepare_rows(source, 0, start, down)
        prepare_rows(source, 1, start, up)
    for sign in range(2):
        for part in range(2):
            sum_ref[sign, part] = products(sign, part, down, f_hi, f_lo)


def high_kernel(own_ref, above_ref, sum_ref, u0, u1, u2, u3, out_ref, f_hi, f_lo, link_ref):
    first_x = lax.axis_index("core") == 0
    multiply_links(own_ref.at[1], above_ref, link_ref)
    transport(own_ref.at[1], above_ref, link_ref, f_hi, f_lo)
    for sign in range(2):
        for part in range(2):
            total = sum_ref[sign, part] + products(sign, part, (u0, u1, u2, u3), f_hi, f_lo)
            for block in range(8):
                for half in range(2):
                    x, y = block % 4, half * 2 + block // 4
                    to = jnp.where(first_x, x * 4 + y, y * 4 + x)
                    for by in range(NZD):
                        out_ref[to, by * 4 + sign * 2 + part] = total[
                            by * LANES + block * 16 : by * LANES + block * 16 + 16,
                            half * LANES : half * LANES + LANES,
                        ]


def gather_kernel(separations_ref, shares_ref, out_ref):
    def one(line, carry):
        fields = []
        for q in range(NZD):
            at = line * 16 + separations_ref[q] * 4
            sums = []
            for index in range(4):
                total = shares_ref[0, at + index]
                for source in range(1, 4):
                    total = total + shares_ref[source, at + index]
                sums.append(total * 0.5)
            plus_real, plus_imag, minus_real, minus_imag = sums
            fields.append(
                [
                    plus_imag - minus_imag,
                    minus_real - plus_real,
                    plus_real + minus_real,
                    plus_imag + minus_imag,
                ]
            )
        for pair in range(2):
            for z, value in enumerate(exchange_pieces(fields[2 * pair] + fields[2 * pair + 1])):
                out_ref[line * 8 + z, pair] = value
        return carry

    lax.fori_loop(0, 4, one, 0, unroll=4)


def place_kernel(own_ref, mirror_ref, out_ref):
    padding = jnp.zeros((LANES - 32, LANES), jnp.float32)
    turned = jnp.concatenate([own_ref[0], own_ref[1], padding]).T
    for pair in range(2):
        for index in range(8):
            q = pair * 2 + index // 4
            g = (index // 2) % 2
            part = index % 2
            out_ref[0, q, g, part] = turned[
                index * 16 : index * 16 + 16, pair * 16 : pair * 16 + 16
            ]
            value = mirror_ref[pair, :, index * 16 : index * 16 + 16]
            out_ref[1, q, g, part] = -value if part else value


SMEM = pl.BlockSpec(memory_space=pltpu.SMEM)
VMEM = pl.BlockSpec(memory_space=pltpu.VMEM)


def call(kernel, outs, inputs, scratch=(), limit=32, flops=0, space=VMEM):
    shapes = [jax.ShapeDtypeStruct(shape, held) for shape, held in outs]
    specs = [SMEM if value.dtype == jnp.int32 else space for value in inputs]
    count = sum(value.size for value in inputs)
    return pl.pallas_call(
        kernel,
        out_shape=shapes,
        in_specs=specs,
        out_specs=[VMEM] * len(outs),
        scratch_shapes=list(scratch),
        compiler_params=pltpu.CompilerParams(vmem_limit_bytes=limit * 1024 * 1024),
        cost_estimate=pl.CostEstimate(flops=flops, bytes_accessed=count * 4, transcendentals=0),
    )(*inputs)


F32, B16 = jnp.float32, jnp.bfloat16
FIELD_SCRATCH = (
    pltpu.VMEM((2, 512, 384), B16),
    pltpu.VMEM((2, 512, 384), B16),
    pltpu.VMEM((72, LANES), F32),
)
LOW_SCRATCH = (pltpu.VMEM((2, 256, 384), B16),) * 4 + FIELD_SCRATCH
FIELD_FLOPS = 2 * 2 * 2 * 3 * 512 * 384 * 256


def position(x, y, core, z):
    return (((y % 2 * 4 + x) * 2 + core) * 8 + z) * 2 + y // 2


def rings(step, with_z):
    groups = []
    for core in range(2):
        for line in range(4):
            rows = []
            for z in range(8):
                if core == step:
                    rows.append([position(i, line, core, z) for i in range(4)])
                else:
                    rows.append([position(line, i, core, z) for i in range(4)])
            if with_z:
                groups.append([row[i] for i in range(4) for row in rows])
            else:
                groups.extend(rows)
    return groups


def exchange(value, groups):
    return lax.all_to_all(
        value, EIG + SPACE, split_axis=0, concat_axis=0, tiled=True, axis_index_groups=groups
    )


def local(eigenvectors, gauge_links, separations):
    vectors = eigenvectors.reshape(1536, LANES)
    links = gauge_links.reshape(72, LANES)
    (chunks,) = call(
        cut_kernel,
        [((16, ROWS, LANES), F32)],
        (vectors, links),
        (
            pltpu.VMEM((1536, LANES), F32),
            pltpu.VMEM((72, LANES), F32),
            pltpu.SemaphoreType.DMA((5,)),
        ),
        limit=56,
        space=pl.BlockSpec(memory_space=pltpu.HBM),
    )
    own = lax.all_to_all(chunks, PLANE, split_axis=0, concat_axis=0, tiled=True)
    own = own.reshape(2, 8, ROWS, LANES)
    above = lax.ppermute(own[0], "z", [(i, (i - 1) % 8) for i in range(8)])
    other = lax.ppermute(own, "core", [(0, 1), (1, 0)])

    low = call(
        low_kernel,
        [((2, 2, 512, 256), F32)] + [((2, 256, 384), B16)] * 4,
        (own, other),
        LOW_SCRATCH,
        flops=FIELD_FLOPS,
    )
    (shares,) = call(
        high_kernel,
        [((16, 16, 16, LANES), F32)],
        (own, above, *low),
        FIELD_SCRATCH,
        flops=FIELD_FLOPS,
    )
    shares = exchange(shares.reshape(4, 64, 16, LANES), rings(0, False))
    (parts,) = call(gather_kernel, [((32, 2, 16, LANES), F32)], (separations, shares))
    parts = exchange(parts, rings(1, True))
    block = jnp.sum(parts, axis=0)
    mirror = lax.ppermute(
        block, EIG + SPACE, [(e * 16 + s, s * 16 + e) for e in range(16) for s in range(16)]
    )
    (fields,) = call(place_kernel, [((2, NZD, 2, 2, 16, 16), F32)], (block, mirror))
    return fields


def solution(mesh):
    fine = Mesh(mesh.devices.reshape([SIZES[name] for name in EIG + SPACE]), EIG + SPACE)
    return jax.shard_map(
        local,
        mesh=fine,
        in_specs=(
            P(None, EIG, None, None, SPACE, None),
            P(None, None, None, SPACE, None),
            P(),
        ),
        out_specs=P(None, None, None, None, SPACE, EIG),
        check_vma=False,
    )
```

```python
import jax
import jax.numpy as jnp
from jax import lax
from jax.experimental import pallas as pl
from jax.experimental.pallas import tpu as pltpu
from jax.sharding import Mesh, PartitionSpec as P

EIG = ("ylo", "x", "core")
SPACE = ("z", "yhi")
PLANE = ("yhi", "ylo", "x")
SIZES = {"ylo": 2, "x": 4, "core": 2, "z": 8, "yhi": 2}

NZD = 4
LANES = 128
PIECE = 16
ROWS = 104


def roll(value, by):
    return pltpu.roll(value, by % LANES, value.ndim - 1)


def lanes_of(value):
    return lax.broadcasted_iota(jnp.int32, value.shape, value.ndim - 1)


def exchange_pieces(rows):
    piece = lanes_of(rows[0]) >> 4
    for bit in (1, 2, 4):
        upper = (piece & bit) != 0
        after = list(rows)
        for i in range(8):
            if i & bit == 0:
                low, high = rows[i], rows[i | bit]
                after[i] = jnp.where(upper, roll(high, 16 * bit), low)
                after[i | bit] = jnp.where(upper, high, roll(low, -16 * bit))
        rows = after
    return rows


def cut_kernel(vectors_hbm, links_hbm, out_ref, vectors_ref, links_ref, arrived):
    copies = [
        pltpu.make_async_copy(vectors_hbm.at[rows], vectors_ref.at[rows], arrived.at[index])
        for index, rows in enumerate(pl.ds(i * 384, 384) for i in (0, 2, 1, 3))
    ]
    copies.append(pltpu.make_async_copy(links_hbm, links_ref, arrived.at[4]))
    for copy in copies:
        copy.start()
    for half in range(2):
        copies[2 * half].wait()
        copies[2 * half + 1].wait()
        for j in range(2):
            for colour in range(3):

                def load(part, spin, plane):
                    first = (((part * 16 + half * 8) * 4 + spin) * 3 + colour) * 4 + plane
                    return vectors_ref[pl.ds(first, 8, stride=48), :]

                plus = [None] * 8
                minus = [None] * 8
                for plane in range(4):
                    upper_real, upper_imag = load(0, j, plane), load(1, j, plane)
                    lower_real, lower_imag = load(0, j + 2, plane), load(1, j + 2, plane)
                    plus[plane] = upper_real - lower_imag
                    plus[4 + plane] = upper_imag + lower_real
                    minus[plane] = upper_real + lower_imag
                    minus[4 + plane] = upper_imag - lower_real
                both = [jnp.stack(pair) for pair in zip(plus, minus)]
                for block, value in enumerate(exchange_pieces(both)):
                    for sign in range(2):
                        first = (sign * 3 + colour) * 16 + half * 8
                        out_ref[j * 8 + block, first : first + 8, :] = value[sign]
    copies[4].wait()
    own = lax.axis_index(("ylo", "x"))
    row = lax.broadcasted_iota(jnp.int32, (8, LANES), 0)
    rows = []
    for part in range(2):
        for plane in range(4):
            mine = links_ref[pl.ds((part * 9 + own) * 4 + plane, 1), :]
            last = links_ref[(part * 9 + 8) * 4 + plane : (part * 9 + 8) * 4 + plane + 1, :]
            rows.append(jnp.where(row == 0, mine, last))
    for block, value in enumerate(exchange_pieces(rows)):
        out_ref[block, 96:104, :] = value
        out_ref[8 + block, 96:104, :] = value


def shifted(here, here_swapped, above, above_swapped, by):
    if by == 4:
        return above, above_swapped
    keep = ((lanes_of(here) >> 4) & 3) >= by
    return (
        roll(jnp.where(keep, here, above_swapped), -16 * by),
        roll(jnp.where(keep, here_swapped, above), -16 * by),
    )


def split(value):
    hi = value.astype(jnp.bfloat16)
    return hi, (value - hi.astype(jnp.float32)).astype(jnp.bfloat16)


def spread_link(entry):
    real_half = lanes_of(entry) < 64
    swapped = roll(entry, 64)
    return jnp.where(real_half, entry, swapped), jnp.where(real_half, -swapped, entry)


def link_rows(source):
    entries = [source[i, 96:97, :] for i in range(8)] + [source[0, 97:98, :]]
    return [[entries[3 * i + j] for j in range(3)] for i in range(3)]


def multiply_links(here_ref, above_ref, link_ref):
    here, above = link_rows(here_ref), link_rows(above_ref)
    here_swapped = [[roll(e, 64) for e in line] for line in here]
    above_swapped = [[roll(e, 64) for e in line] for line in above]
    product = here
    for by in range(1, NZD + 1):
        if by > 1:
            moved = [
                [
                    shifted(here[i][j], here_swapped[i][j], above[i][j], above_swapped[i][j], by - 1)
                    for j in range(3)
                ]
                for i in range(3)
            ]
            product = [
                [
                    sum(
                        factors[i][m][0] * moved[m][j][0] + factors[i][m][1] * moved[m][j][1]
                        for m in range(3)
                    )
                    for j in range(3)
                ]
                for i in range(3)
            ]
        factors = [[spread_link(e) for e in line] for line in product]
        for i in range(3):
            for j in range(3):
                at = ((by - 1) * 9 + i * 3 + j) * 2
                link_ref[at : at + 1, :] = factors[i][j][0]
                link_ref[at + 1 : at + 2, :] = factors[i][j][1]


def transport(sign, here_ref, above_ref, link_ref, hi_ref, lo_ref):
    def one_block(block, carry):
        for _ in range(1):
            here, above, here_swapped, above_swapped = [], [], [], []
            for c in range(3):
                first = (sign * 3 + c) * 16
                here.append(here_ref[block, first : first + 16, :])
                above.append(above_ref[block, first : first + 16, :])
                here_swapped.append(roll(here[c], 64))
                above_swapped.append(roll(above[c], 64))
            for by in range(1, NZD + 1):
                rows = pl.ds(pl.multiple_of((by - 1) * LANES + block * 16, 16), 16)
                moved = [
                    shifted(here[c], here_swapped[c], above[c], above_swapped[c], by)
                    for c in range(3)
                ]
                for i in range(3):
                    total = None
                    for j in range(3):
                        at = ((by - 1) * 9 + i * 3 + j) * 2
                        term = (
                            link_ref[at : at + 1, :] * moved[j][0]
                            + link_ref[at + 1 : at + 2, :] * moved[j][1]
                        )
                        total = term if total is None else total + term
                    hi, lo = split(total)
                    hi_ref[rows, i * LANES : i * LANES + LANES] = hi
                    lo_ref[rows, i * LANES : i * LANES + LANES] = lo
        return carry

    lax.fori_loop(0, 8, one_block, 0, unroll=8)


def prepare_rows(source, half, start, refs):
    start = pl.multiple_of(start, LANES)
    for sign in range(2):
        for colour in range(3):
            first = (sign * 3 + colour) * 16
            value = source[half, :, first : first + 16, :].reshape(LANES, LANES)
            swapped = roll(value, 64)
            turned = jnp.where(lanes_of(value) < 64, -swapped, swapped)
            at = (sign, pl.ds(start, LANES), slice(colour * LANES, colour * LANES + LANES))
            refs[0][at], refs[1][at] = split(value)
            refs[2][at], refs[3][at] = split(turned)


def products(sign, part, rows, hi_ref, lo_ref):
    def product_of(left, right):
        return lax.dot_general(
            left, right, (((1,), (1,)), ((), ())), preferred_element_type=jnp.float32
        )

    rows_hi, rows_lo = rows[2 * part][1 - sign], rows[2 * part + 1][1 - sign]
    both = jnp.concatenate([hi_ref[...], lo_ref[...]], axis=1)
    return product_of(both, jnp.concatenate([rows_hi, rows_hi], axis=1)) + product_of(
        hi_ref[...], rows_lo
    )


def low_kernel(
    own_ref, other_ref, sum_ref, u0, u1, u2, u3, d0, d1, d2, d3, h0, l0, h1, l1, link_ref
):
    cls = lax.axis_index("core")
    down, up = (d0, d1, d2, d3), (u0, u1, u2, u3)
    multiply_links(own_ref.at[0], own_ref.at[1], link_ref)
    for source, start in ((own_ref, cls * LANES), (other_ref, (1 - cls) * LANES)):
        prepare_rows(source, 0, start, down)
        prepare_rows(source, 1, start, up)
    for sign, (hi_ref, lo_ref) in enumerate(((h0, l0), (h1, l1))):
        transport(sign, own_ref.at[0], own_ref.at[1], link_ref, hi_ref, lo_ref)
        for part in range(2):
            sum_ref[sign, part] = products(sign, part, down, hi_ref, lo_ref)


def high_kernel(own_ref, above_ref, sum_ref, u0, u1, u2, u3, out_ref, h0, l0, h1, l1, link_ref):
    first_x = lax.axis_index("core") == 0
    multiply_links(own_ref.at[1], above_ref, link_ref)
    for sign, (hi_ref, lo_ref) in enumerate(((h0, l0), (h1, l1))):
        transport(sign, own_ref.at[1], above_ref, link_ref, hi_ref, lo_ref)
        for part in range(2):
            total = sum_ref[sign, part] + products(sign, part, (u0, u1, u2, u3), hi_ref, lo_ref)
            for block in range(8):
                for half in range(2):
                    x, y = block % 4, half * 2 + block // 4
                    to = jnp.where(first_x, x * 4 + y, y * 4 + x)
                    for by in range(NZD):
                        out_ref[to, by * 4 + sign * 2 + part] = total[
                            by * LANES + block * 16 : by * LANES + block * 16 + 16,
                            half * LANES : half * LANES + LANES,
                        ]


def gather_kernel(separations_ref, shares_ref, out_ref):
    def one(line, carry):
        fields = []
        for q in range(NZD):
            at = line * 16 + separations_ref[q] * 4
            sums = []
            for index in range(4):
                total = shares_ref[0, at + index]
                for source in range(1, 4):
                    total = total + shares_ref[source, at + index]
                sums.append(total * 0.5)
            plus_real, plus_imag, minus_real, minus_imag = sums
            fields.append(
                [
                    plus_imag - minus_imag,
                    minus_real - plus_real,
                    plus_real + minus_real,
                    plus_imag + minus_imag,
                ]
            )
        for pair in range(2):
            turned = jnp.concatenate(fields[2 * pair] + fields[2 * pair + 1]).T
            for z in range(8):
                out_ref[line * 8 + z, pair] = turned[z * 16 : z * 16 + 16]
        return carry

    lax.fori_loop(0, 4, one, 0, unroll=4)


def place_kernel(own_ref, mirror_ref, out_ref):
    padding = jnp.zeros((LANES - 32, LANES), jnp.float32)
    turned = jnp.concatenate([mirror_ref[0], mirror_ref[1], padding]).T
    for pair in range(2):
        for index in range(8):
            q = pair * 2 + index // 4
            g = (index // 2) % 2
            part = index % 2
            out_ref[0, q, g, part] = own_ref[pair, :, index * 16 : index * 16 + 16]
            value = turned[index * 16 : index * 16 + 16, pair * 16 : pair * 16 + 16]
            out_ref[1, q, g, part] = -value if part else value


SMEM = pl.BlockSpec(memory_space=pltpu.SMEM)
VMEM = pl.BlockSpec(memory_space=pltpu.VMEM)


def call(kernel, outs, inputs, scratch=(), limit=32, flops=0, space=VMEM):
    shapes = [jax.ShapeDtypeStruct(shape, held) for shape, held in outs]
    specs = [SMEM if value.dtype == jnp.int32 else space for value in inputs]
    count = sum(value.size for value in inputs)
    return pl.pallas_call(
        kernel,
        out_shape=shapes,
        in_specs=specs,
        out_specs=[VMEM] * len(outs),
        scratch_shapes=list(scratch),
        compiler_params=pltpu.CompilerParams(vmem_limit_bytes=limit * 1024 * 1024),
        cost_estimate=pl.CostEstimate(flops=flops, bytes_accessed=count * 4, transcendentals=0),
    )(*inputs)


F32, B16 = jnp.float32, jnp.bfloat16
FIELD_SCRATCH = (
    pltpu.VMEM((512, 384), B16),
    pltpu.VMEM((512, 384), B16),
    pltpu.VMEM((512, 384), B16),
    pltpu.VMEM((512, 384), B16),
    pltpu.VMEM((72, LANES), F32),
)
LOW_SCRATCH = (pltpu.VMEM((2, 256, 384), B16),) * 4 + FIELD_SCRATCH
FIELD_FLOPS = 2 * 2 * 2 * 3 * 512 * 384 * 256


def position(x, y, core, z):
    return (((y % 2 * 4 + x) * 2 + core) * 8 + z) * 2 + y // 2


def rings(step, with_z):
    groups = []
    for core in range(2):
        for line in range(4):
            rows = []
            for z in range(8):
                if core == step:
                    rows.append([position(i, line, core, z) for i in range(4)])
                else:
                    rows.append([position(line, i, core, z) for i in range(4)])
            if with_z:
                groups.append([row[i] for i in range(4) for row in rows])
            else:
                groups.extend(rows)
    return groups


def exchange(value, groups):
    return lax.all_to_all(
        value, EIG + SPACE, split_axis=0, concat_axis=0, tiled=True, axis_index_groups=groups
    )


def local(eigenvectors, gauge_links, separations):
    vectors = eigenvectors.reshape(1536, LANES)
    links = gauge_links.reshape(72, LANES)
    (chunks,) = call(
        cut_kernel,
        [((16, ROWS, LANES), F32)],
        (vectors, links),
        (
            pltpu.VMEM((1536, LANES), F32),
            pltpu.VMEM((72, LANES), F32),
            pltpu.SemaphoreType.DMA((5,)),
        ),
        limit=56,
        space=pl.BlockSpec(memory_space=pltpu.HBM),
    )
    own = lax.all_to_all(chunks, PLANE, split_axis=0, concat_axis=0, tiled=True)
    own = own.reshape(2, 8, ROWS, LANES)
    above = lax.ppermute(own[0], "z", [(i, (i - 1) % 8) for i in range(8)])
    other = lax.ppermute(own, "core", [(0, 1), (1, 0)])

    low = call(
        low_kernel,
        [((2, 2, 512, 256), F32)] + [((2, 256, 384), B16)] * 4,
        (own, other),
        LOW_SCRATCH,
        flops=FIELD_FLOPS,
    )
    (shares,) = call(
        high_kernel,
        [((16, 16, 16, LANES), F32)],
        (own, above, *low),
        FIELD_SCRATCH,
        flops=FIELD_FLOPS,
    )
    shares = exchange(shares.reshape(4, 64, 16, LANES), rings(0, False))
    (parts,) = call(gather_kernel, [((32, 2, 16, LANES), F32)], (separations, shares))
    parts = exchange(parts, rings(1, True))
    block = jnp.sum(parts, axis=0)
    mirror = lax.ppermute(
        block, EIG + SPACE, [(e * 16 + s, s * 16 + e) for e in range(16) for s in range(16)]
    )
    (fields,) = call(place_kernel, [((2, NZD, 2, 2, 16, 16), F32)], (block, mirror))
    return fields


def solution(mesh):
    fine = Mesh(mesh.devices.reshape([SIZES[name] for name in EIG + SPACE]), EIG + SPACE)
    return jax.shard_map(
        local,
        mesh=fine,
        in_specs=(
            P(None, EIG, None, None, SPACE, None),
            P(None, None, None, SPACE, None),
            P(),
        ),
        out_specs=P(None, None, None, None, SPACE, EIG),
        check_vma=False,
    )
```

```python
import functools

import jax
import jax.numpy as jnp
from jax import lax
from jax.experimental import pallas as pl
from jax.experimental.pallas import tpu as pltpu
from jax.sharding import Mesh, PartitionSpec as P

EIG = ("ylo", "x", "core")
SPACE = ("z", "yhi")
PLANE = ("yhi", "ylo", "x")
SIZES = {"ylo": 2, "x": 4, "core": 2, "z": 8, "yhi": 2}

NZD = 4
LANES = 128
PIECE = 16
ROWS = 104
FIRST = (0, 56)
LINK_ROW = 48


def roll(value, by):
    return pltpu.roll(value, by % LANES, value.ndim - 1)


def lanes_of(value):
    return lax.broadcasted_iota(jnp.int32, value.shape, value.ndim - 1)


def exchange_pieces(rows):
    piece = lanes_of(rows[0]) >> 4
    for bit in (1, 2, 4):
        upper = (piece & bit) != 0
        after = list(rows)
        for i in range(8):
            if i & bit == 0:
                low, high = rows[i], rows[i | bit]
                after[i] = jnp.where(upper, roll(high, 16 * bit), low)
                after[i | bit] = jnp.where(upper, high, roll(low, -16 * bit))
        rows = after
    return rows


def cut_kernel(vectors_hbm, links_hbm, out_ref, vectors_ref, links_ref, arrived):
    copies = [
        pltpu.make_async_copy(vectors_hbm.at[rows], vectors_ref.at[rows], arrived.at[index])
        for index, rows in enumerate(pl.ds(i * 384, 384) for i in (0, 2, 1, 3))
    ]
    copies.append(pltpu.make_async_copy(links_hbm, links_ref, arrived.at[4]))
    for copy in copies:
        copy.start()
    for half in range(2):
        copies[2 * half].wait()
        copies[2 * half + 1].wait()
        for j in range(2):
            for colour in range(3):

                def load(part, spin, plane):
                    first = (((part * 16 + half * 8) * 4 + spin) * 3 + colour) * 4 + plane
                    return vectors_ref[pl.ds(first, 8, stride=48), :]

                plus = [None] * 8
                minus = [None] * 8
                for plane in range(4):
                    upper_real, upper_imag = load(0, j, plane), load(1, j, plane)
                    lower_real, lower_imag = load(0, j + 2, plane), load(1, j + 2, plane)
                    plus[plane] = upper_real - lower_imag
                    plus[4 + plane] = upper_imag + lower_real
                    minus[plane] = upper_real + lower_imag
                    minus[4 + plane] = upper_imag - lower_real
                both = [jnp.stack(pair) for pair in zip(plus, minus)]
                for block, value in enumerate(exchange_pieces(both)):
                    for sign in range(2):
                        first = FIRST[sign] + colour * 16 + half * 8
                        out_ref[j * 8 + block, first : first + 8, :] = value[sign]
    copies[4].wait()
    own = lax.axis_index(("ylo", "x"))
    row = lax.broadcasted_iota(jnp.int32, (8, LANES), 0)
    rows = []
    for part in range(2):
        for plane in range(4):
            mine = links_ref[pl.ds((part * 9 + own) * 4 + plane, 1), :]
            last = links_ref[(part * 9 + 8) * 4 + plane : (part * 9 + 8) * 4 + plane + 1, :]
            rows.append(jnp.where(row == 0, mine, last))
    for block, value in enumerate(exchange_pieces(rows)):
        out_ref[block, LINK_ROW : LINK_ROW + 8, :] = value
        out_ref[8 + block, LINK_ROW : LINK_ROW + 8, :] = value


def shifted(here, here_swapped, above, above_swapped, by):
    if by == 4:
        return above, above_swapped
    keep = ((lanes_of(here) >> 4) & 3) >= by
    return (
        roll(jnp.where(keep, here, above_swapped), -16 * by),
        roll(jnp.where(keep, here_swapped, above), -16 * by),
    )


def split(value):
    hi = value.astype(jnp.bfloat16)
    return hi, (value - hi.astype(jnp.float32)).astype(jnp.bfloat16)


def spread_link(entry):
    real_half = lanes_of(entry) < 64
    swapped = roll(entry, 64)
    return jnp.where(real_half, entry, swapped), jnp.where(real_half, -swapped, entry)


def link_rows(source):
    entries = [source[i, LINK_ROW : LINK_ROW + 1, :] for i in range(8)]
    entries.append(source[0, LINK_ROW + 1 : LINK_ROW + 2, :])
    return [[entries[3 * i + j] for j in range(3)] for i in range(3)]


def multiply_links(here_ref, above_ref, link_ref):
    here, above = link_rows(here_ref), link_rows(above_ref)
    here_swapped = [[roll(e, 64) for e in line] for line in here]
    above_swapped = [[roll(e, 64) for e in line] for line in above]
    product = here
    for by in range(1, NZD + 1):
        if by > 1:
            moved = [
                [
                    shifted(here[i][j], here_swapped[i][j], above[i][j], above_swapped[i][j], by - 1)
                    for j in range(3)
                ]
                for i in range(3)
            ]
            product = [
                [
                    sum(
                        factors[i][m][0] * moved[m][j][0] + factors[i][m][1] * moved[m][j][1]
                        for m in range(3)
                    )
                    for j in range(3)
                ]
                for i in range(3)
            ]
        factors = [[spread_link(e) for e in line] for line in product]
        for i in range(3):
            for j in range(3):
                at = ((by - 1) * 9 + i * 3 + j) * 2
                link_ref[at : at + 1, :] = factors[i][j][0]
                link_ref[at + 1 : at + 2, :] = factors[i][j][1]


def transport(here_ref, above_ref, link_ref, hi_ref, lo_ref):
    def one_block(block, carry):
        here, above, here_swapped, above_swapped = [], [], [], []
        for c in range(3):
            here.append(here_ref[block, c * 16 : c * 16 + 16, :])
            above.append(above_ref[block, c * 16 : c * 16 + 16, :])
            here_swapped.append(roll(here[c], 64))
            above_swapped.append(roll(above[c], 64))
        for by in range(1, NZD + 1):
            rows = pl.ds(pl.multiple_of((by - 1) * LANES + block * 16, 16), 16)
            moved = [
                shifted(here[c], here_swapped[c], above[c], above_swapped[c], by) for c in range(3)
            ]
            for i in range(3):
                total = None
                for j in range(3):
                    at = ((by - 1) * 9 + i * 3 + j) * 2
                    term = (
                        link_ref[at : at + 1, :] * moved[j][0]
                        + link_ref[at + 1 : at + 2, :] * moved[j][1]
                    )
                    total = term if total is None else total + term
                hi, lo = split(total)
                hi_ref[rows, i * LANES : i * LANES + LANES] = hi
                lo_ref[rows, i * LANES : i * LANES + LANES] = lo
        return carry

    lax.fori_loop(0, 8, one_block, 0, unroll=8)


def prepare_rows(source, half, start, refs):
    start = pl.multiple_of(start, LANES)
    for sign in range(2):
        for colour in range(3):
            first = FIRST[sign] + colour * 16
            value = source[half, :, first : first + 16, :].reshape(LANES, LANES)
            swapped = roll(value, 64)
            turned = jnp.where(lanes_of(value) < 64, -swapped, swapped)
            at = (sign, pl.ds(start, LANES), slice(colour * LANES, colour * LANES + LANES))
            refs[0][at], refs[1][at] = split(value)
            refs[2][at], refs[3][at] = split(turned)


def products(sign, part, rows, hi_ref, lo_ref):
    def product_of(left, right):
        return lax.dot_general(
            left, right, (((1,), (1,)), ((), ())), preferred_element_type=jnp.float32
        )

    rows_hi, rows_lo = rows[2 * part][1 - sign], rows[2 * part + 1][1 - sign]
    both = jnp.concatenate([hi_ref[...], lo_ref[...]], axis=1)
    return product_of(both, jnp.concatenate([rows_hi, rows_hi], axis=1)) + product_of(
        hi_ref[...], rows_lo
    )


def low_kernel(own_ref, other_ref, *refs):
    sum_refs, up, down, (hi_ref, lo_ref, link_ref) = refs[:2], refs[2:6], refs[6:10], refs[10:]
    cls = lax.axis_index("core")
    multiply_links(own_ref.at[0], own_ref.at[1], link_ref)
    for source, start in ((own_ref, cls * LANES), (other_ref, (1 - cls) * LANES)):
        prepare_rows(source, 0, start, down)
        prepare_rows(source, 1, start, up)
    for sign in range(2):
        mine = pl.ds(FIRST[sign], 48)
        transport(
            own_ref.at[0, :, mine], own_ref.at[1, :, mine], link_ref, hi_ref.at[sign], lo_ref.at[sign]
        )
        for part in range(2):
            sum_refs[sign][part] = products(sign, part, down, hi_ref.at[sign], lo_ref.at[sign])


def high_kernel(sign, own_ref, above_ref, *refs):
    if sign == 0:
        sum_ref, *up, out_ref, link_ref, hi_ref, lo_ref = refs
        multiply_links(own_ref.at[1], above_ref, link_ref)
    else:
        link_ref, sum_ref, *up, out_ref, hi_ref, lo_ref = refs
    first_x = lax.axis_index("core") == 0
    own_x, own_y = lax.axis_index("x"), lax.axis_index(("yhi", "ylo"))
    transport(own_ref.at[1, :, pl.ds(FIRST[sign], 48)], above_ref, link_ref, hi_ref, lo_ref)
    for part in range(2):
        total = sum_ref[part] + products(sign, part, up, hi_ref, lo_ref)
        for block in range(8):
            for half in range(2):
                x, y = block % 4, half * 2 + block // 4
                to = jnp.where(
                    first_x, lax.rem(x + 4 - own_x, 4) * 4 + y, lax.rem(y + 4 - own_y, 4) * 4 + x
                )
                for by in range(NZD):
                    out_ref[to, by * 2 + part] = total[
                        by * LANES + block * 16 : by * LANES + block * 16 + 16,
                        half * LANES : half * LANES + LANES,
                    ]


def add_kernel(*refs):
    *share_refs, out_ref = refs
    for index in range(32):
        total = share_refs[0][index]
        for share_ref in share_refs[1:]:
            total = total + share_ref[index]
        out_ref[index] = total


def gather_kernel(separations_ref, *refs):
    share_refs, out_ref = (refs[:1], refs[1:5]), refs[5]

    def one(line, carry):
        fields = []
        for q in range(NZD):
            at = line * 8 + separations_ref[q] * 2
            sums = []
            for sign in range(2):
                for part in range(2):
                    total = share_refs[sign][0][at + part]
                    for share_ref in share_refs[sign][1:]:
                        total = total + share_ref[at + part]
                    sums.append(total * 0.5)
            plus_real, plus_imag, minus_real, minus_imag = sums
            fields.append(
                [
                    plus_imag - minus_imag,
                    minus_real - plus_real,
                    plus_real + minus_real,
                    plus_imag + minus_imag,
                ]
            )
        for pair in range(2):
            turned = jnp.concatenate(fields[2 * pair] + fields[2 * pair + 1]).T
            for z in range(8):
                out_ref[line * 8 + z, pair] = turned[z * 16 : z * 16 + 16]
        return carry

    lax.fori_loop(0, 4, one, 0, unroll=4)


def place_kernel(own_ref, mirror_ref, out_ref):
    padding = jnp.zeros((LANES - 32, LANES), jnp.float32)
    turned = jnp.concatenate([mirror_ref[0], mirror_ref[1], padding]).T
    for pair in range(2):
        for index in range(8):
            q = pair * 2 + index // 4
            g = (index // 2) % 2
            part = index % 2
            out_ref[0, q, g, part] = own_ref[pair, :, index * 16 : index * 16 + 16]
            value = turned[index * 16 : index * 16 + 16, pair * 16 : pair * 16 + 16]
            out_ref[1, q, g, part] = -value if part else value


SMEM = pl.BlockSpec(memory_space=pltpu.SMEM)
VMEM = pl.BlockSpec(memory_space=pltpu.VMEM)


def call(kernel, outs, inputs, scratch=(), limit=32, flops=0, space=VMEM):
    shapes = [jax.ShapeDtypeStruct(shape, held) for shape, held in outs]
    specs = [SMEM if value.dtype == jnp.int32 else space for value in inputs]
    count = sum(value.size for value in inputs)
    return pl.pallas_call(
        kernel,
        out_shape=shapes,
        in_specs=specs,
        out_specs=[VMEM] * len(outs),
        scratch_shapes=list(scratch),
        compiler_params=pltpu.CompilerParams(vmem_limit_bytes=limit * 1024 * 1024),
        cost_estimate=pl.CostEstimate(flops=flops, bytes_accessed=count * 4, transcendentals=0),
    )(*inputs)


F32, B16 = jnp.float32, jnp.bfloat16
LINK_SHAPE = ((72, LANES), F32)
FIELD_FLOPS = 2 * 2 * 2 * 3 * 512 * 384 * 256


def position(x, y, core, z):
    return (((y % 2 * 4 + x) * 2 + core) * 8 + z) * 2 + y // 2


def second_groups():
    groups = []
    for line in range(4):
        members = [(i, z) for i in range(4) for z in range(8)]
        groups.append([position(line, i, 0, z) for i, z in members])
        groups.append([position(i, line, 1, z) for i, z in members])
    return groups


def first_shift(value, by):
    pairs = []
    for z in range(8):
        for line in range(4):
            for i in range(4):
                to = (i + by) % 4
                pairs.append((position(i, line, 0, z), position(to, line, 0, z)))
                pairs.append((position(line, i, 1, z), position(line, to, 1, z)))
    return lax.ppermute(value, EIG + SPACE, pairs)


def along_first_ring(shares):
    shares = shares.reshape(4, 32, 16, LANES)
    return [shares[0]] + [first_shift(shares[by], by) for by in (2, 1, 3)]


def exchange(value, groups):
    return lax.all_to_all(
        value, EIG + SPACE, split_axis=0, concat_axis=0, tiled=True, axis_index_groups=groups
    )


def local(eigenvectors, gauge_links, separations):
    vectors = eigenvectors.reshape(1536, LANES)
    links = gauge_links.reshape(72, LANES)
    (chunks,) = call(
        cut_kernel,
        [((16, ROWS, LANES), F32)],
        (vectors, links),
        (
            pltpu.VMEM((1536, LANES), F32),
            pltpu.VMEM((72, LANES), F32),
            pltpu.SemaphoreType.DMA((5,)),
        ),
        limit=56,
        space=pl.BlockSpec(memory_space=pltpu.HBM),
    )
    own = lax.all_to_all(chunks, PLANE, split_axis=0, concat_axis=0, tiled=True)
    own = own.reshape(2, 8, ROWS, LANES)

    def from_above(value):
        return lax.ppermute(value, "z", [(i, (i - 1) % 8) for i in range(8)])

    above = [from_above(own[0, :, : FIRST[1]]), from_above(own[0, :, FIRST[1] :])]
    other = lax.ppermute(own, "core", [(0, 1), (1, 0)])
    plus, minus, *rows = call(
        low_kernel,
        [((2, 512, 256), F32)] * 2 + [((2, 256, 384), B16)] * 4,
        (own, other),
        [pltpu.VMEM((2, 256, 384), B16)] * 4
        + [pltpu.VMEM((2, 512, 384), B16)] * 2
        + [pltpu.VMEM(*LINK_SHAPE)],
        flops=FIELD_FLOPS,
    )
    half_scratch = [pltpu.VMEM((512, 384), B16)] * 2
    shares, links = call(
        functools.partial(high_kernel, 0),
        [((16, 8, 16, LANES), F32), LINK_SHAPE],
        (own, above[0], plus, *rows),
        half_scratch,
        flops=FIELD_FLOPS // 2,
    )
    (summed,) = call(
        add_kernel, [((32, 16, LANES), F32)], along_first_ring(shares), flops=4 * FIELD_FLOPS
    )
    (shares,) = call(
        functools.partial(high_kernel, 1),
        [((16, 8, 16, LANES), F32)],
        (own, above[1], links, minus, *rows),
        half_scratch,
        flops=FIELD_FLOPS // 2,
    )
    summands = [summed] + along_first_ring(shares)
    (parts,) = call(gather_kernel, [((32, 2, 16, LANES), F32)], (separations, *summands))
    parts = exchange(parts, second_groups())
    block = jnp.sum(parts, axis=0)
    mirror = lax.ppermute(
        block, EIG + SPACE, [(e * 16 + s, s * 16 + e) for e in range(16) for s in range(16)]
    )
    (fields,) = call(place_kernel, [((2, NZD, 2, 2, 16, 16), F32)], (block, mirror))
    return fields


def solution(mesh):
    fine = Mesh(mesh.devices.reshape([SIZES[name] for name in EIG + SPACE]), EIG + SPACE)
    return jax.shard_map(
        local,
        mesh=fine,
        in_specs=(
            P(None, EIG, None, None, SPACE, None),
            P(None, None, None, SPACE, None),
            P(),
        ),
        out_specs=P(None, None, None, None, SPACE, EIG),
        check_vma=False,
    )
```

```python
import functools

import jax
import jax.numpy as jnp
from jax import lax
from jax.experimental import pallas as pl
from jax.experimental.pallas import tpu as pltpu
from jax.sharding import Mesh, PartitionSpec as P

EIG = ("ylo", "x", "core")
SPACE = ("z", "yhi")
PLANE = ("yhi", "ylo", "x")
SIZES = {"ylo": 2, "x": 4, "core": 2, "z": 8, "yhi": 2}

NZD = 4
LANES = 128
PIECE = 16
ROWS = 104
FIRST = (0, 56)
LINK_ROW = 48


def roll(value, by):
    return pltpu.roll(value, by % LANES, value.ndim - 1)


def lanes_of(value):
    return lax.broadcasted_iota(jnp.int32, value.shape, value.ndim - 1)


def exchange_pieces(rows):
    piece = lanes_of(rows[0]) >> 4
    for bit in (1, 2, 4):
        upper = (piece & bit) != 0
        after = list(rows)
        for i in range(8):
            if i & bit == 0:
                low, high = rows[i], rows[i | bit]
                after[i] = jnp.where(upper, roll(high, 16 * bit), low)
                after[i | bit] = jnp.where(upper, high, roll(low, -16 * bit))
        rows = after
    return rows


def cut_kernel(vectors_hbm, links_hbm, out_ref, vectors_ref, links_ref, arrived):
    copies = [
        pltpu.make_async_copy(vectors_hbm.at[rows], vectors_ref.at[rows], arrived.at[index])
        for index, rows in enumerate(pl.ds(i * 384, 384) for i in (0, 2, 1, 3))
    ]
    copies.append(pltpu.make_async_copy(links_hbm, links_ref, arrived.at[4]))
    for copy in copies:
        copy.start()
    for half in range(2):
        copies[2 * half].wait()
        copies[2 * half + 1].wait()
        for j in range(2):
            for colour in range(3):

                def load(part, spin, plane):
                    first = (((part * 16 + half * 8) * 4 + spin) * 3 + colour) * 4 + plane
                    return vectors_ref[pl.ds(first, 8, stride=48), :]

                plus = [None] * 8
                minus = [None] * 8
                for plane in range(4):
                    upper_real, upper_imag = load(0, j, plane), load(1, j, plane)
                    lower_real, lower_imag = load(0, j + 2, plane), load(1, j + 2, plane)
                    plus[plane] = upper_real - lower_imag
                    plus[4 + plane] = upper_imag + lower_real
                    minus[plane] = upper_real + lower_imag
                    minus[4 + plane] = upper_imag - lower_real
                both = [jnp.stack(pair) for pair in zip(plus, minus)]
                for block, value in enumerate(exchange_pieces(both)):
                    for sign in range(2):
                        first = FIRST[sign] + colour * 16 + half * 8
                        out_ref[j * 8 + block, first : first + 8, :] = value[sign]
    copies[4].wait()
    own = lax.axis_index(("ylo", "x"))
    row = lax.broadcasted_iota(jnp.int32, (8, LANES), 0)
    rows = []
    for part in range(2):
        for plane in range(4):
            mine = links_ref[pl.ds((part * 9 + own) * 4 + plane, 1), :]
            last = links_ref[(part * 9 + 8) * 4 + plane : (part * 9 + 8) * 4 + plane + 1, :]
            rows.append(jnp.where(row == 0, mine, last))
    for block, value in enumerate(exchange_pieces(rows)):
        out_ref[block, LINK_ROW : LINK_ROW + 8, :] = value
        out_ref[8 + block, LINK_ROW : LINK_ROW + 8, :] = value


def shifted(here, here_swapped, above, above_swapped, by):
    if by == 4:
        return above, above_swapped
    keep = ((lanes_of(here) >> 4) & 3) >= by
    return (
        roll(jnp.where(keep, here, above_swapped), -16 * by),
        roll(jnp.where(keep, here_swapped, above), -16 * by),
    )


def split(value):
    hi = value.astype(jnp.bfloat16)
    return hi, (value - hi.astype(jnp.float32)).astype(jnp.bfloat16)


def spread_link(entry):
    real_half = lanes_of(entry) < 64
    swapped = roll(entry, 64)
    return jnp.where(real_half, entry, swapped), jnp.where(real_half, -swapped, entry)


def link_rows(source):
    entries = [source[i, LINK_ROW : LINK_ROW + 1, :] for i in range(8)]
    entries.append(source[0, LINK_ROW + 1 : LINK_ROW + 2, :])
    return [[entries[3 * i + j] for j in range(3)] for i in range(3)]


def multiply_links(here_ref, above_ref, link_ref):
    here, above = link_rows(here_ref), link_rows(above_ref)
    here_swapped = [[roll(e, 64) for e in line] for line in here]
    above_swapped = [[roll(e, 64) for e in line] for line in above]
    product = here
    for by in range(1, NZD + 1):
        if by > 1:
            moved = [
                [
                    shifted(here[i][j], here_swapped[i][j], above[i][j], above_swapped[i][j], by - 1)
                    for j in range(3)
                ]
                for i in range(3)
            ]
            product = [
                [
                    sum(
                        factors[i][m][0] * moved[m][j][0] + factors[i][m][1] * moved[m][j][1]
                        for m in range(3)
                    )
                    for j in range(3)
                ]
                for i in range(3)
            ]
        factors = [[spread_link(e) for e in line] for line in product]
        for i in range(3):
            for j in range(3):
                at = ((by - 1) * 9 + i * 3 + j) * 2
                link_ref[at : at + 1, :] = factors[i][j][0]
                link_ref[at + 1 : at + 2, :] = factors[i][j][1]


def transport(here_ref, above_ref, link_ref, hi_ref, lo_ref):
    def one_block(block, carry):
        here, above, here_swapped, above_swapped = [], [], [], []
        for c in range(3):
            here.append(here_ref[block, c * 16 : c * 16 + 16, :])
            above.append(above_ref[block, c * 16 : c * 16 + 16, :])
            here_swapped.append(roll(here[c], 64))
            above_swapped.append(roll(above[c], 64))
        for by in range(1, NZD + 1):
            rows = pl.ds(pl.multiple_of((by - 1) * LANES + block * 16, 16), 16)
            moved = [
                shifted(here[c], here_swapped[c], above[c], above_swapped[c], by) for c in range(3)
            ]
            for i in range(3):
                total = None
                for j in range(3):
                    at = ((by - 1) * 9 + i * 3 + j) * 2
                    term = (
                        link_ref[at : at + 1, :] * moved[j][0]
                        + link_ref[at + 1 : at + 2, :] * moved[j][1]
                    )
                    total = term if total is None else total + term
                hi, lo = split(total)
                hi_ref[rows, i * LANES : i * LANES + LANES] = hi
                lo_ref[rows, i * LANES : i * LANES + LANES] = lo
        return carry

    lax.fori_loop(0, 8, one_block, 0, unroll=8)


def prepare_rows(source, half, start, refs):
    start = pl.multiple_of(start, LANES)
    for sign in range(2):
        for colour in range(3):
            first = FIRST[sign] + colour * 16
            value = source[half, :, first : first + 16, :].reshape(LANES, LANES)
            swapped = roll(value, 64)
            turned = jnp.where(lanes_of(value) < 64, -swapped, swapped)
            at = (sign, pl.ds(start, LANES), slice(colour * LANES, colour * LANES + LANES))
            refs[0][at], refs[1][at] = split(value)
            refs[2][at], refs[3][at] = split(turned)


def products(sign, part, rows, hi_ref, lo_ref):
    def product_of(left, right):
        return lax.dot_general(
            left, right, (((1,), (1,)), ((), ())), preferred_element_type=jnp.float32
        )

    rows_hi, rows_lo = rows[2 * part][1 - sign], rows[2 * part + 1][1 - sign]
    both = jnp.concatenate([hi_ref[...], lo_ref[...]], axis=1)
    return product_of(both, jnp.concatenate([rows_hi, rows_hi], axis=1)) + product_of(
        hi_ref[...], rows_lo
    )


def low_kernel(own_ref, other_ref, *refs):
    sum_refs, up, down, (hi_ref, lo_ref, link_ref) = refs[:2], refs[2:6], refs[6:10], refs[10:]
    cls = lax.axis_index("core")
    multiply_links(own_ref.at[0], own_ref.at[1], link_ref)
    for source, start in ((own_ref, cls * LANES), (other_ref, (1 - cls) * LANES)):
        prepare_rows(source, 0, start, down)
        prepare_rows(source, 1, start, up)
    for sign in range(2):
        mine = pl.ds(FIRST[sign], 48)
        transport(
            own_ref.at[0, :, mine], own_ref.at[1, :, mine], link_ref, hi_ref.at[sign], lo_ref.at[sign]
        )
        for part in range(2):
            sum_refs[sign][part] = products(sign, part, down, hi_ref.at[sign], lo_ref.at[sign])


def high_kernel(sign, own_ref, above_ref, *refs):
    if sign == 0:
        sum_ref, *up, out_ref, link_ref, hi_ref, lo_ref = refs
        multiply_links(own_ref.at[1], above_ref, link_ref)
    else:
        link_ref, sum_ref, *up, out_ref, hi_ref, lo_ref = refs
    first_x = lax.axis_index("core") == 0
    own_x, own_y = lax.axis_index("x"), lax.axis_index(("yhi", "ylo"))
    transport(own_ref.at[1, :, pl.ds(FIRST[sign], 48)], above_ref, link_ref, hi_ref, lo_ref)
    for part in range(2):
        total = sum_ref[part] + products(sign, part, up, hi_ref, lo_ref)
        for block in range(8):
            for half in range(2):
                x, y = block % 4, half * 2 + block // 4
                to = jnp.where(
                    first_x, lax.rem(x + 4 - own_x, 4) * 4 + y, lax.rem(y + 4 - own_y, 4) * 4 + x
                )
                for by in range(NZD):
                    out_ref[to, by * 2 + part] = total[
                        by * LANES + block * 16 : by * LANES + block * 16 + 16,
                        half * LANES : half * LANES + LANES,
                    ]


def add_kernel(*refs):
    *share_refs, out_ref = refs
    for index in range(32):
        total = share_refs[0][index]
        for share_ref in share_refs[1:]:
            total = total + share_ref[index]
        out_ref[index] = total


def gather_kernel(order_ref, *refs):
    share_refs, out_ref = (refs[:1], refs[1:5]), refs[5]

    def one(line, carry):
        fields = []
        for q in range(NZD):
            at = line * 8 + order_ref[q]
            sums = []
            for sign in range(2):
                for part in range(2):
                    total = share_refs[sign][0][at + part]
                    for share_ref in share_refs[sign][1:]:
                        total = total + share_ref[at + part]
                    sums.append(total * 0.5)
            plus_real, plus_imag, minus_real, minus_imag = sums
            fields.append(
                [
                    plus_imag - minus_imag,
                    minus_real - plus_real,
                    plus_real + minus_real,
                    plus_imag + minus_imag,
                ]
            )
        for pair in range(2):
            turned = jnp.concatenate(fields[2 * pair] + fields[2 * pair + 1]).T
            for z in range(8):
                out_ref[line * 8 + z, pair] = turned[z * 16 : z * 16 + 16]
        return carry

    lax.fori_loop(0, 4, one, 0, unroll=4)


def place_kernel(own_ref, mirror_ref, out_ref):
    padding = jnp.zeros((LANES - 32, LANES), jnp.float32)
    turned = jnp.concatenate([mirror_ref[0], mirror_ref[1], padding]).T
    for pair in range(2):
        for index in range(8):
            q = pair * 2 + index // 4
            g = (index // 2) % 2
            part = index % 2
            out_ref[0, q, g, part] = own_ref[pair, :, index * 16 : index * 16 + 16]
            value = turned[index * 16 : index * 16 + 16, pair * 16 : pair * 16 + 16]
            out_ref[1, q, g, part] = -value if part else value


SMEM = pl.BlockSpec(memory_space=pltpu.SMEM)
VMEM = pl.BlockSpec(memory_space=pltpu.VMEM)


def call(kernel, outs, inputs, scratch=(), limit=32, flops=0, space=VMEM):
    shapes = [jax.ShapeDtypeStruct(shape, held) for shape, held in outs]
    specs = [SMEM if value.dtype == jnp.int32 else space for value in inputs]
    count = sum(value.size for value in inputs)
    return pl.pallas_call(
        kernel,
        out_shape=shapes,
        in_specs=specs,
        out_specs=[VMEM] * len(outs),
        scratch_shapes=list(scratch),
        compiler_params=pltpu.CompilerParams(vmem_limit_bytes=limit * 1024 * 1024),
        cost_estimate=pl.CostEstimate(flops=flops, bytes_accessed=count * 4, transcendentals=0),
    )(*inputs)


F32, B16 = jnp.float32, jnp.bfloat16
LINK_SHAPE = ((72, LANES), F32)
FIELD_FLOPS = 2 * 2 * 2 * 3 * 512 * 384 * 256


def position(x, y, core, z):
    return (((y % 2 * 4 + x) * 2 + core) * 8 + z) * 2 + y // 2


def second_groups():
    groups = []
    for line in range(4):
        members = [(i, z) for i in range(4) for z in range(8)]
        groups.append([position(line, i, 0, z) for i, z in members])
        groups.append([position(i, line, 1, z) for i, z in members])
    return groups


def first_shift(value, by):
    pairs = []
    for z in range(8):
        for line in range(4):
            for i in range(4):
                to = (i + by) % 4
                pairs.append((position(i, line, 0, z), position(to, line, 0, z)))
                pairs.append((position(line, i, 1, z), position(line, to, 1, z)))
    return lax.ppermute(value, EIG + SPACE, pairs)


def along_first_ring(shares):
    shares = shares.reshape(4, 32, 16, LANES)
    return [shares[0]] + [first_shift(shares[by], by) for by in (2, 1, 3)]


def exchange(value, groups):
    return lax.all_to_all(
        value, EIG + SPACE, split_axis=0, concat_axis=0, tiled=True, axis_index_groups=groups
    )


def local(eigenvectors, gauge_links, separations):
    vectors = eigenvectors.reshape(1536, LANES)
    links = gauge_links.reshape(72, LANES)
    (chunks,) = call(
        cut_kernel,
        [((16, ROWS, LANES), F32)],
        (vectors, links),
        (
            pltpu.VMEM((1536, LANES), F32),
            pltpu.VMEM((72, LANES), F32),
            pltpu.SemaphoreType.DMA((5,)),
        ),
        limit=56,
        space=pl.BlockSpec(memory_space=pltpu.HBM),
    )
    own = lax.all_to_all(chunks, PLANE, split_axis=0, concat_axis=0, tiled=True)
    own = own.reshape(2, 8, ROWS, LANES)

    def from_above(value):
        return lax.ppermute(value, "z", [(i, (i - 1) % 8) for i in range(8)])

    above = [from_above(own[0, :, : FIRST[1]]), from_above(own[0, :, FIRST[1] :])]
    other = lax.ppermute(own, "core", [(0, 1), (1, 0)])
    plus, minus, *rows = call(
        low_kernel,
        [((2, 512, 256), F32)] * 2 + [((2, 256, 384), B16)] * 4,
        (own, other),
        [pltpu.VMEM((2, 256, 384), B16)] * 4
        + [pltpu.VMEM((2, 512, 384), B16)] * 2
        + [pltpu.VMEM(*LINK_SHAPE)],
        flops=FIELD_FLOPS,
    )
    half_scratch = [pltpu.VMEM((512, 384), B16)] * 2
    shares, links = call(
        functools.partial(high_kernel, 0),
        [((16, 8, 16, LANES), F32), LINK_SHAPE],
        (own, above[0], plus, *rows),
        half_scratch,
        flops=FIELD_FLOPS // 2,
    )
    (summed,) = call(
        add_kernel, [((32, 16, LANES), F32)], along_first_ring(shares), flops=4 * FIELD_FLOPS
    )
    (shares,) = call(
        functools.partial(high_kernel, 1),
        [((16, 8, 16, LANES), F32)],
        (own, above[1], links, minus, *rows),
        half_scratch,
        flops=FIELD_FLOPS // 2,
    )
    summands = [summed] + along_first_ring(shares)
    (parts,) = call(gather_kernel, [((32, 2, 16, LANES), F32)], (separations * 2, *summands))
    parts = exchange(parts, second_groups())
    block = jnp.sum(parts, axis=0)
    mirror = lax.ppermute(
        block, EIG + SPACE, [(e * 16 + s, s * 16 + e) for e in range(16) for s in range(16)]
    )
    (fields,) = call(place_kernel, [((2, NZD, 2, 2, 16, 16), F32)], (block, mirror))
    return fields


def solution(mesh):
    fine = Mesh(mesh.devices.reshape([SIZES[name] for name in EIG + SPACE]), EIG + SPACE)
    return jax.shard_map(
        local,
        mesh=fine,
        in_specs=(
            P(None, EIG, None, None, SPACE, None),
            P(None, None, None, SPACE, None),
            P(),
        ),
        out_specs=P(None, None, None, None, SPACE, EIG),
        check_vma=False,
    )
```

```python
import functools

import jax
import jax.numpy as jnp
from jax import lax
from jax.experimental import pallas as pl
from jax.experimental.pallas import tpu as pltpu
from jax.sharding import Mesh, PartitionSpec as P

EIG = ("ylo", "x", "core")
SPACE = ("z", "yhi")
PLANE = ("yhi", "ylo", "x")
SIZES = {"ylo": 2, "x": 4, "core": 2, "z": 8, "yhi": 2}

NZD = 4
LANES = 128
PIECE = 16
ROWS = 104
FIRST = (0, 56)
LINK_ROW = 48


def roll(value, by):
    return pltpu.roll(value, by % LANES, value.ndim - 1)


def lanes_of(value):
    return lax.broadcasted_iota(jnp.int32, value.shape, value.ndim - 1)


def exchange_pieces(rows):
    piece = lanes_of(rows[0]) >> 4
    for bit in (1, 2, 4):
        upper = (piece & bit) != 0
        after = list(rows)
        for i in range(8):
            if i & bit == 0:
                low, high = rows[i], rows[i | bit]
                after[i] = jnp.where(upper, roll(high, 16 * bit), low)
                after[i | bit] = jnp.where(upper, high, roll(low, -16 * bit))
        rows = after
    return rows


def cut_kernel(vectors_hbm, links_hbm, out_hbm, vectors_ref, links_ref, out_ref, arrived, left):
    copies = [
        pltpu.make_async_copy(vectors_hbm.at[rows], vectors_ref.at[rows], arrived.at[index])
        for index, rows in enumerate(pl.ds(i * 384, 384) for i in (0, 2, 1, 3))
    ]
    copies.append(pltpu.make_async_copy(links_hbm, links_ref, arrived.at[4]))
    for copy in copies:
        copy.start()
    leaving = []

    def send(first):
        rows = (slice(None), pl.ds(first, 8))
        leaving.append(
            pltpu.make_async_copy(out_ref.at[rows], out_hbm.at[rows], left.at[len(leaving)])
        )
        leaving[-1].start()

    for half in range(2):
        copies[2 * half].wait()
        copies[2 * half + 1].wait()
        for colour in range(3):
            for j in range(2):

                def load(part, spin, plane):
                    first = (((part * 16 + half * 8) * 4 + spin) * 3 + colour) * 4 + plane
                    return vectors_ref[pl.ds(first, 8, stride=48), :]

                plus = [None] * 8
                minus = [None] * 8
                for plane in range(4):
                    upper_real, upper_imag = load(0, j, plane), load(1, j, plane)
                    lower_real, lower_imag = load(0, j + 2, plane), load(1, j + 2, plane)
                    plus[plane] = upper_real - lower_imag
                    plus[4 + plane] = upper_imag + lower_real
                    minus[plane] = upper_real + lower_imag
                    minus[4 + plane] = upper_imag - lower_real
                both = [jnp.stack(pair) for pair in zip(plus, minus)]
                for block, value in enumerate(exchange_pieces(both)):
                    for sign in range(2):
                        first = FIRST[sign] + colour * 16 + half * 8
                        out_ref[j * 8 + block, first : first + 8, :] = value[sign]
            for sign in range(2):
                send(FIRST[sign] + colour * 16 + half * 8)
        if half == 0:
            copies[4].wait()
            own = lax.axis_index(("ylo", "x"))
            row = lax.broadcasted_iota(jnp.int32, (8, LANES), 0)
            rows = []
            for part in range(2):
                for plane in range(4):
                    mine = links_ref[pl.ds((part * 9 + own) * 4 + plane, 1), :]
                    at = (part * 9 + 8) * 4 + plane
                    rows.append(jnp.where(row == 0, mine, links_ref[at : at + 1, :]))
            for block, value in enumerate(exchange_pieces(rows)):
                out_ref[block, LINK_ROW : LINK_ROW + 8, :] = value
                out_ref[8 + block, LINK_ROW : LINK_ROW + 8, :] = value
            send(LINK_ROW)
    for copy in leaving:
        copy.wait()


def shifted(here, here_swapped, above, above_swapped, by):
    if by == 4:
        return above, above_swapped
    keep = ((lanes_of(here) >> 4) & 3) >= by
    return (
        roll(jnp.where(keep, here, above_swapped), -16 * by),
        roll(jnp.where(keep, here_swapped, above), -16 * by),
    )


def split(value):
    hi = value.astype(jnp.bfloat16)
    return hi, (value - hi.astype(jnp.float32)).astype(jnp.bfloat16)


def spread_link(entry):
    real_half = lanes_of(entry) < 64
    swapped = roll(entry, 64)
    return jnp.where(real_half, entry, swapped), jnp.where(real_half, -swapped, entry)


def link_rows(source):
    entries = [source[i, LINK_ROW : LINK_ROW + 1, :] for i in range(8)]
    entries.append(source[0, LINK_ROW + 1 : LINK_ROW + 2, :])
    return [[entries[3 * i + j] for j in range(3)] for i in range(3)]


def multiply_links(here_ref, above_ref, link_ref):
    here, above = link_rows(here_ref), link_rows(above_ref)
    here_swapped = [[roll(e, 64) for e in line] for line in here]
    above_swapped = [[roll(e, 64) for e in line] for line in above]
    product = here
    for by in range(1, NZD + 1):
        if by > 1:
            moved = [
                [
                    shifted(here[i][j], here_swapped[i][j], above[i][j], above_swapped[i][j], by - 1)
                    for j in range(3)
                ]
                for i in range(3)
            ]
            product = [
                [
                    sum(
                        factors[i][m][0] * moved[m][j][0] + factors[i][m][1] * moved[m][j][1]
                        for m in range(3)
                    )
                    for j in range(3)
                ]
                for i in range(3)
            ]
        factors = [[spread_link(e) for e in line] for line in product]
        for i in range(3):
            for j in range(3):
                at = ((by - 1) * 9 + i * 3 + j) * 2
                link_ref[at : at + 1, :] = factors[i][j][0]
                link_ref[at + 1 : at + 2, :] = factors[i][j][1]


def transport(here_ref, above_ref, link_ref, hi_ref, lo_ref):
    def one_block(block, carry):
        here, above, here_swapped, above_swapped = [], [], [], []
        for c in range(3):
            here.append(here_ref[block, c * 16 : c * 16 + 16, :])
            above.append(above_ref[block, c * 16 : c * 16 + 16, :])
            here_swapped.append(roll(here[c], 64))
            above_swapped.append(roll(above[c], 64))
        for by in range(1, NZD + 1):
            rows = pl.ds(pl.multiple_of((by - 1) * LANES + block * 16, 16), 16)
            moved = [
                shifted(here[c], here_swapped[c], above[c], above_swapped[c], by) for c in range(3)
            ]
            for i in range(3):
                total = None
                for j in range(3):
                    at = ((by - 1) * 9 + i * 3 + j) * 2
                    term = (
                        link_ref[at : at + 1, :] * moved[j][0]
                        + link_ref[at + 1 : at + 2, :] * moved[j][1]
                    )
                    total = term if total is None else total + term
                hi, lo = split(total)
                hi_ref[rows, i * LANES : i * LANES + LANES] = hi
                lo_ref[rows, i * LANES : i * LANES + LANES] = lo
        return carry

    lax.fori_loop(0, 8, one_block, 0, unroll=8)


def prepare_rows(source, half, start, refs):
    start = pl.multiple_of(start, LANES)
    for sign in range(2):
        for colour in range(3):
            first = FIRST[sign] + colour * 16
            value = source[half, :, first : first + 16, :].reshape(LANES, LANES)
            swapped = roll(value, 64)
            turned = jnp.where(lanes_of(value) < 64, -swapped, swapped)
            at = (sign, pl.ds(start, LANES), slice(colour * LANES, colour * LANES + LANES))
            refs[0][at], refs[1][at] = split(value)
            refs[2][at], refs[3][at] = split(turned)


def products(sign, part, rows, hi_ref, lo_ref):
    def product_of(left, right):
        return lax.dot_general(
            left, right, (((1,), (1,)), ((), ())), preferred_element_type=jnp.float32
        )

    rows_hi, rows_lo = rows[2 * part][1 - sign], rows[2 * part + 1][1 - sign]
    both = jnp.concatenate([hi_ref[...], lo_ref[...]], axis=1)
    return product_of(both, jnp.concatenate([rows_hi, rows_hi], axis=1)) + product_of(
        hi_ref[...], rows_lo
    )


def low_kernel(own_ref, other_ref, *refs):
    sum_refs, up, down, (hi_ref, lo_ref, link_ref) = refs[:2], refs[2:6], refs[6:10], refs[10:]
    cls = lax.axis_index("core")
    multiply_links(own_ref.at[0], own_ref.at[1], link_ref)
    for source, start in ((own_ref, cls * LANES), (other_ref, (1 - cls) * LANES)):
        prepare_rows(source, 0, start, down)
        prepare_rows(source, 1, start, up)
    for sign in range(2):
        mine = pl.ds(FIRST[sign], 48)
        transport(
            own_ref.at[0, :, mine], own_ref.at[1, :, mine], link_ref, hi_ref.at[sign], lo_ref.at[sign]
        )
        for part in range(2):
            sum_refs[sign][part] = products(sign, part, down, hi_ref.at[sign], lo_ref.at[sign])


def high_kernel(sign, own_ref, above_ref, *refs):
    if sign == 0:
        sum_ref, *up, out_ref, link_ref, hi_ref, lo_ref = refs
        multiply_links(own_ref.at[1], above_ref, link_ref)
    else:
        link_ref, sum_ref, *up, out_ref, hi_ref, lo_ref = refs
    first_x = lax.axis_index("core") == 0
    own_x, own_y = lax.axis_index("x"), lax.axis_index(("yhi", "ylo"))
    transport(own_ref.at[1, :, pl.ds(FIRST[sign], 48)], above_ref, link_ref, hi_ref, lo_ref)
    for part in range(2):
        total = sum_ref[part] + products(sign, part, up, hi_ref, lo_ref)
        for block in range(8):
            for half in range(2):
                x, y = block % 4, half * 2 + block // 4
                to = jnp.where(
                    first_x, lax.rem(x + 4 - own_x, 4) * 4 + y, lax.rem(y + 4 - own_y, 4) * 4 + x
                )
                for by in range(NZD):
                    out_ref[to, by * 2 + part] = total[
                        by * LANES + block * 16 : by * LANES + block * 16 + 16,
                        half * LANES : half * LANES + LANES,
                    ]


def add_kernel(separations_ref, *refs):
    *share_refs, out_ref, order_ref = refs
    for index in range(32):
        total = share_refs[0][index]
        for share_ref in share_refs[1:]:
            total = total + share_ref[index]
        out_ref[index] = total
    row = lax.broadcasted_iota(jnp.int32, (8, LANES), 0)
    order = jnp.zeros((8, LANES), jnp.int32)
    for q in range(NZD):
        order = jnp.where(row == q, separations_ref[q], order)
    order_ref[...] = order


def gather_kernel(order_ref, *refs):
    share_refs, out_ref = (refs[:1], refs[1:5]), refs[5]
    chosen = [[order_ref[q : q + 1, :] == k for k in range(NZD - 1)] for q in range(NZD)]

    def one(line, carry):
        by_length = []
        for k in range(NZD):
            sums = []
            for sign in range(2):
                for part in range(2):
                    at = line * 8 + k * 2 + part
                    total = share_refs[sign][0][at]
                    for share_ref in share_refs[sign][1:]:
                        total = total + share_ref[at]
                    sums.append(total * 0.5)
            plus_real, plus_imag, minus_real, minus_imag = sums
            by_length.append(
                [
                    plus_imag - minus_imag,
                    minus_real - plus_real,
                    plus_real + minus_real,
                    plus_imag + minus_imag,
                ]
            )
        fields = []
        for q in range(NZD):
            field = by_length[NZD - 1]
            for k in range(NZD - 1):
                field = [
                    jnp.where(chosen[q][k], one_length, other)
                    for one_length, other in zip(by_length[k], field)
                ]
            fields.append(field)
        for pair in range(2):
            turned = jnp.concatenate(fields[2 * pair] + fields[2 * pair + 1]).T
            for z in range(8):
                out_ref[line * 8 + z, pair] = turned[z * 16 : z * 16 + 16]
        return carry

    lax.fori_loop(0, 4, one, 0, unroll=4)


def place_kernel(own_ref, mirror_ref, out_ref):
    padding = jnp.zeros((LANES - 32, LANES), jnp.float32)
    turned = jnp.concatenate([mirror_ref[0], mirror_ref[1], padding]).T
    for pair in range(2):
        for index in range(8):
            q = pair * 2 + index // 4
            g = (index // 2) % 2
            part = index % 2
            out_ref[0, q, g, part] = own_ref[pair, :, index * 16 : index * 16 + 16]
            value = turned[index * 16 : index * 16 + 16, pair * 16 : pair * 16 + 16]
            out_ref[1, q, g, part] = -value if part else value


SMEM = pl.BlockSpec(memory_space=pltpu.SMEM)
VMEM = pl.BlockSpec(memory_space=pltpu.VMEM)


def call(kernel, outs, inputs, scratch=(), limit=32, flops=0, space=VMEM):
    shapes = [jax.ShapeDtypeStruct(shape, held) for shape, held in outs]
    specs = [SMEM if value.shape == (NZD,) else space for value in inputs]
    count = sum(value.size for value in inputs)
    return pl.pallas_call(
        kernel,
        out_shape=shapes,
        in_specs=specs,
        out_specs=[space] * len(outs),
        scratch_shapes=list(scratch),
        compiler_params=pltpu.CompilerParams(vmem_limit_bytes=limit * 1024 * 1024),
        cost_estimate=pl.CostEstimate(flops=flops, bytes_accessed=count * 4, transcendentals=0),
    )(*inputs)


F32, B16 = jnp.float32, jnp.bfloat16
LINK_SHAPE = ((72, LANES), F32)
FIELD_FLOPS = 2 * 2 * 2 * 3 * 512 * 384 * 256


def position(x, y, core, z):
    return (((y % 2 * 4 + x) * 2 + core) * 8 + z) * 2 + y // 2


def second_groups():
    groups = []
    for line in range(4):
        members = [(i, z) for i in range(4) for z in range(8)]
        groups.append([position(line, i, 0, z) for i, z in members])
        groups.append([position(i, line, 1, z) for i, z in members])
    return groups


def first_shift(value, by):
    pairs = []
    for z in range(8):
        for line in range(4):
            for i in range(4):
                to = (i + by) % 4
                pairs.append((position(i, line, 0, z), position(to, line, 0, z)))
                pairs.append((position(line, i, 1, z), position(line, to, 1, z)))
    return lax.ppermute(value, EIG + SPACE, pairs)


def along_first_ring(shares):
    shares = shares.reshape(4, 32, 16, LANES)
    return [shares[0]] + [first_shift(shares[by], by) for by in (2, 1, 3)]


def exchange(value, groups):
    return lax.all_to_all(
        value, EIG + SPACE, split_axis=0, concat_axis=0, tiled=True, axis_index_groups=groups
    )


def local(eigenvectors, gauge_links, separations):
    vectors = eigenvectors.reshape(1536, LANES)
    links = gauge_links.reshape(72, LANES)
    (chunks,) = call(
        cut_kernel,
        [((16, ROWS, LANES), F32)],
        (vectors, links),
        (
            pltpu.VMEM((1584, LANES), F32),
            pltpu.VMEM((72, LANES), F32),
            pltpu.VMEM((16, ROWS, LANES), F32),
            pltpu.SemaphoreType.DMA((5,)),
            pltpu.SemaphoreType.DMA((13,)),
        ),
        limit=56,
        space=pl.BlockSpec(memory_space=pltpu.HBM),
    )
    own = lax.all_to_all(chunks, PLANE, split_axis=0, concat_axis=0, tiled=True)
    own = own.reshape(2, 8, ROWS, LANES)

    def from_above(value):
        return lax.ppermute(value, "z", [(i, (i - 1) % 8) for i in range(8)])

    above = [from_above(own[0, :, : FIRST[1]]), from_above(own[0, :, FIRST[1] :])]
    other = lax.ppermute(own, "core", [(0, 1), (1, 0)])
    plus, minus, *rows = call(
        low_kernel,
        [((2, 512, 256), F32)] * 2 + [((2, 256, 384), B16)] * 4,
        (own, other),
        [pltpu.VMEM((2, 256, 384), B16)] * 4
        + [pltpu.VMEM((2, 512, 384), B16)] * 2
        + [pltpu.VMEM(*LINK_SHAPE)],
        flops=FIELD_FLOPS,
    )
    half_scratch = [pltpu.VMEM((512, 384), B16)] * 2
    shares, links = call(
        functools.partial(high_kernel, 0),
        [((16, 8, 16, LANES), F32), LINK_SHAPE],
        (own, above[0], plus, *rows),
        half_scratch,
        flops=FIELD_FLOPS // 2,
    )
    summed, order = call(
        add_kernel,
        [((32, 16, LANES), F32), ((8, LANES), jnp.int32)],
        (separations, *along_first_ring(shares)),
        flops=4 * FIELD_FLOPS,
    )
    (shares,) = call(
        functools.partial(high_kernel, 1),
        [((16, 8, 16, LANES), F32)],
        (own, above[1], links, minus, *rows),
        half_scratch,
        flops=FIELD_FLOPS // 2,
    )
    summands = [summed] + along_first_ring(shares)
    (parts,) = call(gather_kernel, [((32, 2, 16, LANES), F32)], (order, *summands))
    parts = exchange(parts, second_groups())
    block = jnp.sum(parts, axis=0)
    mirror = lax.ppermute(
        block, EIG + SPACE, [(e * 16 + s, s * 16 + e) for e in range(16) for s in range(16)]
    )
    (fields,) = call(place_kernel, [((2, NZD, 2, 2, 16, 16), F32)], (block, mirror))
    return fields


def solution(mesh):
    fine = Mesh(mesh.devices.reshape([SIZES[name] for name in EIG + SPACE]), EIG + SPACE)
    return jax.shard_map(
        local,
        mesh=fine,
        in_specs=(
            P(None, EIG, None, None, SPACE, None),
            P(None, None, None, SPACE, None),
            P(),
        ),
        out_specs=P(None, None, None, None, SPACE, EIG),
        check_vma=False,
    )
```

```python
import functools

import jax
import jax.numpy as jnp
from jax import lax
from jax.experimental import pallas as pl
from jax.experimental.pallas import tpu as pltpu
from jax.sharding import Mesh, PartitionSpec as P

EIG = ("ylo", "x", "core")
SPACE = ("z", "yhi")
PLANE = ("yhi", "ylo", "x")
SIZES = {"ylo": 2, "x": 4, "core": 2, "z": 8, "yhi": 2}

NZD = 4
LANES = 128
PIECE = 16
ROWS = 104
FIRST = (0, 56)
LINK_ROW = 48


def roll(value, by):
    return pltpu.roll(value, by % LANES, value.ndim - 1)


def lanes_of(value):
    return lax.broadcasted_iota(jnp.int32, value.shape, value.ndim - 1)


def exchange_pieces(rows):
    piece = lanes_of(rows[0]) >> 4
    for bit in (1, 2, 4):
        upper = (piece & bit) != 0
        after = list(rows)
        for i in range(8):
            if i & bit == 0:
                low, high = rows[i], rows[i | bit]
                after[i] = jnp.where(upper, roll(high, 16 * bit), low)
                after[i | bit] = jnp.where(upper, high, roll(low, -16 * bit))
        rows = after
    return rows


def cut_kernel(vectors_hbm, links_hbm, out_hbm, vectors_ref, links_ref, out_ref, arrived, left):
    copies = [
        pltpu.make_async_copy(vectors_hbm.at[rows], vectors_ref.at[rows], arrived.at[index])
        for index, rows in enumerate(pl.ds(i * 384, 384) for i in (0, 2, 1, 3))
    ]
    copies.append(pltpu.make_async_copy(links_hbm, links_ref, arrived.at[4]))
    for copy in copies:
        copy.start()
    leaving = []

    def send(first):
        rows = (slice(None), pl.ds(first, 8))
        leaving.append(
            pltpu.make_async_copy(out_ref.at[rows], out_hbm.at[rows], left.at[len(leaving)])
        )
        leaving[-1].start()

    for half in range(2):
        copies[2 * half].wait()
        copies[2 * half + 1].wait()
        for colour in range(3):
            for j in range(2):

                def load(part, spin, plane):
                    first = (((part * 16 + half * 8) * 4 + spin) * 3 + colour) * 4 + plane
                    return vectors_ref[pl.ds(first, 8, stride=48), :]

                plus = [None] * 8
                minus = [None] * 8
                for plane in range(4):
                    upper_real, upper_imag = load(0, j, plane), load(1, j, plane)
                    lower_real, lower_imag = load(0, j + 2, plane), load(1, j + 2, plane)
                    plus[plane] = upper_real - lower_imag
                    plus[4 + plane] = upper_imag + lower_real
                    minus[plane] = upper_real + lower_imag
                    minus[4 + plane] = upper_imag - lower_real
                both = [jnp.stack(pair) for pair in zip(plus, minus)]
                for block, value in enumerate(exchange_pieces(both)):
                    for sign in range(2):
                        first = FIRST[sign] + colour * 16 + half * 8
                        out_ref[j * 8 + block, first : first + 8, :] = value[sign]
            for sign in range(2):
                send(FIRST[sign] + colour * 16 + half * 8)
        if half == 0:
            copies[4].wait()
            own = lax.axis_index(("ylo", "x"))
            row = lax.broadcasted_iota(jnp.int32, (8, LANES), 0)
            rows = []
            for part in range(2):
                for plane in range(4):
                    mine = links_ref[pl.ds((part * 9 + own) * 4 + plane, 1), :]
                    at = (part * 9 + 8) * 4 + plane
                    rows.append(jnp.where(row == 0, mine, links_ref[at : at + 1, :]))
            for block, value in enumerate(exchange_pieces(rows)):
                out_ref[block, LINK_ROW : LINK_ROW + 8, :] = value
                out_ref[8 + block, LINK_ROW : LINK_ROW + 8, :] = value
            send(LINK_ROW)
    for copy in leaving:
        copy.wait()


def shifted(here, here_swapped, above, above_swapped, by):
    if by == 4:
        return above, above_swapped
    keep = ((lanes_of(here) >> 4) & 3) >= by
    return (
        roll(jnp.where(keep, here, above_swapped), -16 * by),
        roll(jnp.where(keep, here_swapped, above), -16 * by),
    )


def split(value):
    hi = value.astype(jnp.bfloat16)
    return hi, (value - hi.astype(jnp.float32)).astype(jnp.bfloat16)


def spread_link(entry):
    real_half = lanes_of(entry) < 64
    swapped = roll(entry, 64)
    return jnp.where(real_half, entry, swapped), jnp.where(real_half, -swapped, entry)


def link_rows(source):
    entries = [source[i, LINK_ROW : LINK_ROW + 1, :] for i in range(8)]
    entries.append(source[0, LINK_ROW + 1 : LINK_ROW + 2, :])
    return [[entries[3 * i + j] for j in range(3)] for i in range(3)]


def multiply_links(here_ref, above_ref, link_ref):
    here, above = link_rows(here_ref), link_rows(above_ref)
    here_swapped = [[roll(e, 64) for e in line] for line in here]
    above_swapped = [[roll(e, 64) for e in line] for line in above]
    product = here
    for by in range(1, NZD + 1):
        if by > 1:
            moved = [
                [
                    shifted(here[i][j], here_swapped[i][j], above[i][j], above_swapped[i][j], by - 1)
                    for j in range(3)
                ]
                for i in range(3)
            ]
            product = [
                [
                    sum(
                        factors[i][m][0] * moved[m][j][0] + factors[i][m][1] * moved[m][j][1]
                        for m in range(3)
                    )
                    for j in range(3)
                ]
                for i in range(3)
            ]
        factors = [[spread_link(e) for e in line] for line in product]
        for i in range(3):
            for j in range(3):
                at = ((by - 1) * 9 + i * 3 + j) * 2
                link_ref[at : at + 1, :] = factors[i][j][0]
                link_ref[at + 1 : at + 2, :] = factors[i][j][1]


def transport(here_ref, above_ref, link_ref, hi_ref, lo_ref):
    def one_block(block, carry):
        here, above, here_swapped, above_swapped = [], [], [], []
        for c in range(3):
            here.append(here_ref[block, c * 16 : c * 16 + 16, :])
            above.append(above_ref[block, c * 16 : c * 16 + 16, :])
            here_swapped.append(roll(here[c], 64))
            above_swapped.append(roll(above[c], 64))
        for by in range(1, NZD + 1):
            rows = pl.ds(pl.multiple_of((by - 1) * LANES + block * 16, 16), 16)
            moved = [
                shifted(here[c], here_swapped[c], above[c], above_swapped[c], by) for c in range(3)
            ]
            for i in range(3):
                total = None
                for j in range(3):
                    at = ((by - 1) * 9 + i * 3 + j) * 2
                    term = (
                        link_ref[at : at + 1, :] * moved[j][0]
                        + link_ref[at + 1 : at + 2, :] * moved[j][1]
                    )
                    total = term if total is None else total + term
                hi, lo = split(total)
                hi_ref[rows, i * LANES : i * LANES + LANES] = hi
                lo_ref[rows, i * LANES : i * LANES + LANES] = lo
        return carry

    lax.fori_loop(0, 8, one_block, 0, unroll=8)


def prepare_rows(source, half, start, refs):
    start = pl.multiple_of(start, LANES)
    for sign in range(2):
        for colour in range(3):
            first = FIRST[sign] + colour * 16
            value = source[half, :, first : first + 16, :].reshape(LANES, LANES)
            swapped = roll(value, 64)
            turned = jnp.where(lanes_of(value) < 64, -swapped, swapped)
            at = (sign, pl.ds(start, LANES), slice(colour * LANES, colour * LANES + LANES))
            refs[0][at], refs[1][at] = split(value)
            refs[2][at], refs[3][at] = split(turned)


def products(sign, part, rows, hi_ref, lo_ref):
    def product_of(left, right):
        return lax.dot_general(
            left, right, (((1,), (1,)), ((), ())), preferred_element_type=jnp.float32
        )

    rows_hi, rows_lo = rows[2 * part][1 - sign], rows[2 * part + 1][1 - sign]
    both = jnp.concatenate([hi_ref[...], lo_ref[...]], axis=1)
    return product_of(both, jnp.concatenate([rows_hi, rows_hi], axis=1)) + product_of(
        hi_ref[...], rows_lo
    )


def low_kernel(own_ref, other_ref, *refs):
    sum_refs, up, down, (hi_ref, lo_ref, link_ref) = refs[:2], refs[2:6], refs[6:10], refs[10:]
    cls = lax.axis_index("core")
    multiply_links(own_ref.at[0], own_ref.at[1], link_ref)
    for source, start in ((own_ref, cls * LANES), (other_ref, (1 - cls) * LANES)):
        prepare_rows(source, 0, start, down)
        prepare_rows(source, 1, start, up)
    for sign in range(2):
        mine = pl.ds(FIRST[sign], 48)
        transport(
            own_ref.at[0, :, mine], own_ref.at[1, :, mine], link_ref, hi_ref.at[sign], lo_ref.at[sign]
        )
        for part in range(2):
            sum_refs[sign][part] = products(sign, part, down, hi_ref.at[sign], lo_ref.at[sign])


def high_kernel(sign, own_ref, above_ref, *refs):
    if sign == 0:
        sum_ref, *up, out_ref, link_ref, hi_ref, lo_ref = refs
        multiply_links(own_ref.at[1], above_ref, link_ref)
    else:
        link_ref, sum_ref, *up, out_ref, hi_ref, lo_ref = refs
    first_x = lax.axis_index("core") == 0
    own_x, own_y = lax.axis_index("x"), lax.axis_index(("yhi", "ylo"))
    transport(own_ref.at[1, :, pl.ds(FIRST[sign], 48)], above_ref, link_ref, hi_ref, lo_ref)
    for part in range(2):
        total = sum_ref[part] + products(sign, part, up, hi_ref, lo_ref)
        for block in range(8):
            for half in range(2):
                x, y = block % 4, half * 2 + block // 4
                to = jnp.where(
                    first_x, lax.rem(x + 4 - own_x, 4) * 4 + y, lax.rem(y + 4 - own_y, 4) * 4 + x
                )
                for by in range(NZD):
                    out_ref[to, by * 2 + part] = total[
                        by * LANES + block * 16 : by * LANES + block * 16 + 16,
                        half * LANES : half * LANES + LANES,
                    ]


def add_kernel(separations_ref, *refs):
    *share_refs, out_ref, order_ref = refs
    for index in range(32):
        total = share_refs[0][index]
        for share_ref in share_refs[1:]:
            total = total + share_ref[index]
        out_ref[index] = total
    row = lax.broadcasted_iota(jnp.int32, (8, LANES), 0)
    order = jnp.zeros((8, LANES), jnp.int32)
    for q in range(NZD):
        order = jnp.where(row == q, separations_ref[q], order)
    order_ref[...] = order


def gather_kernel(order_ref, *refs):
    share_refs, out_ref = (refs[:1], refs[1:5]), refs[5]
    chosen = [[order_ref[q : q + 1, :] == k for k in range(NZD - 1)] for q in range(NZD)]

    def one(line, carry):
        by_length = []
        for k in range(NZD):
            sums = []
            for sign in range(2):
                for part in range(2):
                    at = line * 8 + k * 2 + part
                    total = share_refs[sign][0][at]
                    for share_ref in share_refs[sign][1:]:
                        total = total + share_ref[at]
                    sums.append(total * 0.5)
            plus_real, plus_imag, minus_real, minus_imag = sums
            by_length.append(
                [
                    plus_imag - minus_imag,
                    minus_real - plus_real,
                    plus_real + minus_real,
                    plus_imag + minus_imag,
                ]
            )
        fields = []
        for q in range(NZD):
            field = by_length[NZD - 1]
            for k in range(NZD - 1):
                field = [
                    jnp.where(chosen[q][k], one_length, other)
                    for one_length, other in zip(by_length[k], field)
                ]
            fields.append(field)
        for pair in range(2):
            turned = jnp.concatenate(fields[2 * pair] + fields[2 * pair + 1]).T
            for z in range(8):
                out_ref[line * 8 + z, pair] = turned[z * 16 : z * 16 + 16]
        return carry

    lax.fori_loop(0, 4, one, 0, unroll=4)


def forward_kernel(own_ref, out_hbm, held_ref, sent):
    for pair in range(2):
        for index in range(8):
            held_ref[pair * 2 + index // 4, (index // 2) % 2, index % 2] = own_ref[
                pair, :, index * 16 : index * 16 + 16
            ]
    copy = pltpu.make_async_copy(held_ref, out_hbm.at[0], sent.at[0])
    copy.start()
    copy.wait()


def mirror_kernel(mirror_ref, _, out_hbm, held_ref, sent):
    padding = jnp.zeros((LANES - 32, LANES), jnp.float32)
    turned = jnp.concatenate([mirror_ref[0], mirror_ref[1], padding]).T
    for pair in range(2):
        for index in range(8):
            value = turned[index * 16 : index * 16 + 16, pair * 16 : pair * 16 + 16]
            held_ref[pair * 2 + index // 4, (index // 2) % 2, index % 2] = (
                -value if index % 2 else value
            )
    copy = pltpu.make_async_copy(held_ref, out_hbm.at[1], sent.at[0])
    copy.start()
    copy.wait()


def place(kernel, inputs, aliases):
    hbm = pl.BlockSpec(memory_space=pltpu.HBM)
    return pl.pallas_call(
        kernel,
        out_shape=jax.ShapeDtypeStruct((2, NZD, 2, 2, 16, 16), F32),
        in_specs=[VMEM, hbm][: len(inputs)],
        out_specs=hbm,
        scratch_shapes=[pltpu.VMEM((NZD, 2, 2, 16, 16), F32), pltpu.SemaphoreType.DMA((1,))],
        input_output_aliases=aliases,
        compiler_params=pltpu.CompilerParams(vmem_limit_bytes=32 * 1024 * 1024),
    )(*inputs)


SMEM = pl.BlockSpec(memory_space=pltpu.SMEM)
VMEM = pl.BlockSpec(memory_space=pltpu.VMEM)


def call(kernel, outs, inputs, scratch=(), limit=32, flops=0, space=VMEM):
    shapes = [jax.ShapeDtypeStruct(shape, held) for shape, held in outs]
    specs = [SMEM if value.shape == (NZD,) else space for value in inputs]
    count = sum(value.size for value in inputs)
    return pl.pallas_call(
        kernel,
        out_shape=shapes,
        in_specs=specs,
        out_specs=[space] * len(outs),
        scratch_shapes=list(scratch),
        compiler_params=pltpu.CompilerParams(vmem_limit_bytes=limit * 1024 * 1024),
        cost_estimate=pl.CostEstimate(flops=flops, bytes_accessed=count * 4, transcendentals=0),
    )(*inputs)


F32, B16 = jnp.float32, jnp.bfloat16
LINK_SHAPE = ((72, LANES), F32)
FIELD_FLOPS = 2 * 2 * 2 * 3 * 512 * 384 * 256


def position(x, y, core, z):
    return (((y % 2 * 4 + x) * 2 + core) * 8 + z) * 2 + y // 2


def second_groups():
    groups = []
    for line in range(4):
        members = [(i, z) for i in range(4) for z in range(8)]
        groups.append([position(line, i, 0, z) for i, z in members])
        groups.append([position(i, line, 1, z) for i, z in members])
    return groups


def first_shift(value, by):
    pairs = []
    for z in range(8):
        for line in range(4):
            for i in range(4):
                to = (i + by) % 4
                pairs.append((position(i, line, 0, z), position(to, line, 0, z)))
                pairs.append((position(line, i, 1, z), position(line, to, 1, z)))
    return lax.ppermute(value, EIG + SPACE, pairs)


def along_first_ring(shares):
    shares = shares.reshape(4, 32, 16, LANES)
    return [shares[0]] + [first_shift(shares[by], by) for by in (2, 1, 3)]


def exchange(value, groups):
    return lax.all_to_all(
        value, EIG + SPACE, split_axis=0, concat_axis=0, tiled=True, axis_index_groups=groups
    )


def local(eigenvectors, gauge_links, separations):
    vectors = eigenvectors.reshape(1536, LANES)
    links = gauge_links.reshape(72, LANES)
    (chunks,) = call(
        cut_kernel,
        [((16, ROWS, LANES), F32)],
        (vectors, links),
        (
            pltpu.VMEM((1584, LANES), F32),
            pltpu.VMEM((72, LANES), F32),
            pltpu.VMEM((16, ROWS, LANES), F32),
            pltpu.SemaphoreType.DMA((5,)),
            pltpu.SemaphoreType.DMA((13,)),
        ),
        limit=56,
        space=pl.BlockSpec(memory_space=pltpu.HBM),
    )
    own = lax.all_to_all(chunks, PLANE, split_axis=0, concat_axis=0, tiled=True)
    own = own.reshape(2, 8, ROWS, LANES)

    def from_above(value):
        return lax.ppermute(value, "z", [(i, (i - 1) % 8) for i in range(8)])

    above = [from_above(own[0, :, : FIRST[1]]), from_above(own[0, :, FIRST[1] :])]
    other = lax.ppermute(own, "core", [(0, 1), (1, 0)])
    plus, minus, *rows = call(
        low_kernel,
        [((2, 512, 256), F32)] * 2 + [((2, 256, 384), B16)] * 4,
        (own, other),
        [pltpu.VMEM((2, 256, 384), B16)] * 4
        + [pltpu.VMEM((2, 512, 384), B16)] * 2
        + [pltpu.VMEM(*LINK_SHAPE)],
        flops=FIELD_FLOPS,
    )
    half_scratch = [pltpu.VMEM((512, 384), B16)] * 2
    shares, links = call(
        functools.partial(high_kernel, 0),
        [((16, 8, 16, LANES), F32), LINK_SHAPE],
        (own, above[0], plus, *rows),
        half_scratch,
        flops=FIELD_FLOPS // 2,
    )
    summed, order = call(
        add_kernel,
        [((32, 16, LANES), F32), ((8, LANES), jnp.int32)],
        (separations, *along_first_ring(shares)),
        flops=4 * FIELD_FLOPS,
    )
    (shares,) = call(
        functools.partial(high_kernel, 1),
        [((16, 8, 16, LANES), F32)],
        (own, above[1], links, minus, *rows),
        half_scratch,
        flops=FIELD_FLOPS // 2,
    )
    summands = [summed] + along_first_ring(shares)
    (parts,) = call(gather_kernel, [((32, 2, 16, LANES), F32)], (order, *summands))
    parts = exchange(parts, second_groups())
    block = jnp.sum(parts, axis=0)
    mirror = lax.ppermute(
        block, EIG + SPACE, [(e * 16 + s, s * 16 + e) for e in range(16) for s in range(16)]
    )
    forward = place(forward_kernel, (block,), {})
    return place(mirror_kernel, (mirror, forward), {1: 0})


def solution(mesh):
    fine = Mesh(mesh.devices.reshape([SIZES[name] for name in EIG + SPACE]), EIG + SPACE)
    return jax.shard_map(
        local,
        mesh=fine,
        in_specs=(
            P(None, EIG, None, None, SPACE, None),
            P(None, None, None, SPACE, None),
            P(),
        ),
        out_specs=P(None, None, None, None, SPACE, EIG),
        check_vma=False,
    )
```
